128 devices in a mesh: gx: 8 (over x, core), gy: 16 (over z, y).
Axes of the slice: x: 4, y: 4, z: 4, core: 2. Of those that a mesh axis runs over, the one named last changes fastest.
Arguments:
- tracers: float32 [12, 48, 512, 1024], P(None, None, 'gy', 'gx'), may hold values from -6 to 6
- level_counts: int32 [512, 1024], P('gy', 'gx'), may hold values from 0 to 48, as said below
- u_vel: float32 [48, 512, 1024], P(None, 'gy', 'gx'), may hold values from -1 to 1
- v_vel: float32 [48, 512, 1024], P(None, 'gy', 'gx'), may hold values from -1 to 1
- diff_depth: float32 [48], replicated, may hold values from 0.25 to 1
- diff_lat: float32 [512], P('gy'), may hold values from 0.05 to 0.2
- thickness: float32 [48], replicated, may hold values from 0.5 to 2
- surface_forcing: float32 [512, 1024], P('gy', 'gx')
- initial_pressure: float32 [512, 1024], P('gy', 'gx'), may hold values from -3 to 3
Outputs:
- new_tracers: float32 [12, 48, 512, 1024], P(None, None, 'gy', 'gx')
- surface_pressure: float32 [512, 1024], P('gy', 'gx')
- pressure_gradient: float32 [2, 512, 1024], P(None, 'gy', 'gx')
The draws below stay inside these ranges and needn't reach their ends.
Inputs may be any that keep to these rules, and one draw needn't show every extreme that they name: level_counts gives each column's number of active levels; 0 marks land.
All inputs are finite; a program needn't handle non-finite values.
Results may differ from the reference program's by a relative error of at most 0.0003.
Values sent between devices are 32-bit elements; how exact they have to be, the bound alone decides.
No kernel may reach another device: no remote copies, remote signals or barrier semaphores. Data moves between devices by JAX's collectives and lax.ppermute only.
A program may use at most 192 MiB of HBM per device.

```python
import math
import jax
import jax.numpy as jnp
from jax import lax

NT = 12
NZ = 48
CX = 128
CY = 32
ITERS = 4
NX = 1024
NY = 512


def draw_level_counts(key, part):
    key = jax.random.fold_in(key, 11)
    node_key, rough_key = jax.random.split(key)
    node_rows = NY // CY + 1
    node_cols = NX // CX + 1
    nodes = jax.random.randint(node_key, (node_rows, node_cols), -(NZ // 2), NZ + NZ // 2 + 1, dtype=jnp.int32)
    lat_index = jnp.arange(NY, dtype=jnp.int32)
    lon_index = jnp.arange(NX, dtype=jnp.int32)
    lat_block = lat_index // CY
    lat_frac = (lat_index % CY)[:, None]
    lon_block = lon_index // CX
    lon_frac = (lon_index % CX)[None, :]
    south_west = nodes[lat_block][:, lon_block]
    south_east = nodes[lat_block][:, lon_block + 1]
    north_west = nodes[lat_block + 1][:, lon_block]
    north_east = nodes[lat_block + 1][:, lon_block + 1]
    total = south_west * (CY - lat_frac) * (CX - lon_frac) + south_east * (CY - lat_frac) * lon_frac + north_west * lat_frac * (CX - lon_frac) + north_east * lat_frac * lon_frac
    smooth = total // (CY * CX)
    rough = jax.random.randint(rough_key, (NY, NX), -2, 3, dtype=jnp.int32)
    return jnp.clip(smooth + rough, 0, NZ).astype(jnp.int32)


def draw_surface_forcing(key, part):
    key = jax.random.fold_in(key, 7)
    rough = jax.random.normal(key, (NY, NX), jnp.float32)
    return rough


def shard_levels(key, shape, cuts, least, largest):
    gain, own = 1.0, jax.random.fold_in(key, 6)
    for axis_at, shards_of in cuts:
        heights = jnp.exp(jax.random.uniform(jax.random.fold_in(own, axis_at), (shards_of,), jnp.float32, least / len(cuts), largest / len(cuts)))
        gain = gain * jnp.repeat(heights, shape[axis_at] // shards_of).reshape([-1 if axis == axis_at else 1 for axis in range(len(shape))])
    return gain


def gaussian(key, dims, width, limit, cuts=(), held_as=jnp.bfloat16):
    result = width * jax.random.normal(key, dims, jnp.float32)
    if cuts:
        result = result * shard_levels(key, dims, cuts, -0.22, 0.18)
    return jnp.clip(result, -limit, limit).astype(held_as)


def setup_inputs(seed: int = 0) -> dict:
    keys = jax.random.split(jax.random.key(seed), 10)
    tracers = gaussian(keys[0], (NT, NZ, NY, NX), 1.0, 6.0, ((2, 16), (3, 8)), jnp.float32)
    level_counts = draw_level_counts(jax.random.fold_in(keys[9], 71), 0)
    u_vel = gaussian(keys[2], (NZ, NY, NX), 0.25, 1.0, ((1, 16), (2, 8)), jnp.float32)
    v_vel = gaussian(keys[3], (NZ, NY, NX), 0.25, 1.0, ((1, 16), (2, 8)), jnp.float32)
    diff_depth = jnp.clip(jnp.exp(jax.random.uniform(keys[4], (NZ,), jnp.float32, math.log(0.25), math.log(1.0))), 0.25, 1.0)
    diff_lat = jnp.clip(jnp.exp(math.log(0.2) - 1.3862944 * jax.random.uniform(keys[5], (NY,), jnp.float32) ** shard_levels(keys[5], (NY,), ((0, 16),), -0.2, 0.2)), 0.05, 0.2)
    thickness = jnp.clip(jnp.exp(jax.random.uniform(keys[6], (NZ,), jnp.float32, math.log(0.5), math.log(2.0))), 0.5, 2.0)
    surface_forcing = draw_surface_forcing(jax.random.fold_in(keys[9], 71), 0)
    initial_pressure = gaussian(keys[8], (NY, NX), 0.5, 3.0, ((0, 16), (1, 8)), jnp.float32)
    return dict(tracers=tracers, level_counts=level_counts, u_vel=u_vel, v_vel=v_vel, diff_depth=diff_depth, diff_lat=diff_lat, thickness=thickness, surface_forcing=surface_forcing, initial_pressure=initial_pressure)


thermal_coef = 0.2
haline_coef = 0.8


def tracer_step(field_pad, active_pad, mixing, u_vel, v_vel, lat_cells, lon_cells):
    def window(values, lat_step, lon_step):
        return values[..., 2 + lat_step:2 + lat_step + lat_cells, 2 + lon_step:2 + lon_step + lon_cells]

    center = window(field_pad, 0, 0)
    active = window(active_pad, 0, 0)

    def seen(lat_step, lon_step):
        nearby = window(active_pad, lat_step, lon_step)
        return nearby * window(field_pad, lat_step, lon_step) + (1.0 - nearby) * center

    to_east = seen(0, 1)
    to_west = seen(0, -1)
    to_north = seen(1, 0)
    to_south = seen(-1, 0)
    grad_x = (8.0 * (to_east - to_west) - (seen(0, 2) - seen(0, -2))) / 12.0
    grad_y = (8.0 * (to_north - to_south) - (seen(2, 0) - seen(-2, 0))) / 12.0
    spread = mixing * (to_east + to_west + to_north + to_south - 4.0 * center)
    return center + active * (spread - u_vel * grad_x - v_vel * grad_y)


def inner_window(values, lat_step, lon_step):
    return values[1 + lat_step:values.shape[0] - 1 + lat_step, 1 + lon_step:values.shape[1] - 1 + lon_step]


def barotropic(values_pad, ocean_pad, center):
    middle = inner_window(values_pad, 0, 0)
    ocean = inner_window(ocean_pad, 0, 0)

    def masked(lat_step, lon_step):
        return inner_window(ocean_pad, lat_step, lon_step) * inner_window(values_pad, lat_step, lon_step)

    edges = masked(0, 1) + masked(0, -1) + masked(1, 0) + masked(-1, 0)
    corners = masked(1, 1) + masked(1, -1) + masked(-1, 1) + masked(-1, -1)
    return ocean * (center * middle - edges - 0.25 * corners) + (1.0 - ocean) * middle


def slope(pressure_pad, ocean_pad):
    ocean = inner_window(ocean_pad, 0, 0)

    def masked(lat_step, lon_step):
        return inner_window(ocean_pad, lat_step, lon_step) * inner_window(pressure_pad, lat_step, lon_step)

    east_part = ocean * 0.5 * (masked(0, 1) - masked(0, -1))
    north_part = ocean * 0.5 * (masked(1, 0) - masked(-1, 0))
    return jnp.stack([east_part, north_part])


def reference(tracers, level_counts, u_vel, v_vel, diff_depth, diff_lat, thickness, surface_forcing, initial_pressure):
    lat_cells, lon_cells = NY, NX
    counts_pad = jnp.pad(level_counts, 2)
    levels = jnp.arange(NZ, dtype=jnp.int32)
    active_pad = (levels[:, None, None] < counts_pad[None]).astype(jnp.float32)
    mixing = diff_depth[:, None, None] * diff_lat[None, :, None]

    def advance(tracer_field):
        padded = jnp.pad(tracer_field, ((0, 0), (2, 2), (2, 2)))
        return tracer_step(padded, active_pad, mixing, u_vel, v_vel, lat_cells, lon_cells)

    new_tracers = lax.map(advance, tracers)
    active = active_pad[:, 2:-2, 2:-2]
    ocean = (level_counts > 0).astype(jnp.float32)
    weights = active * thickness[:, None, None]
    buoyancy = thermal_coef * new_tracers[0] - haline_coef * new_tracers[1]
    forcing = ocean * (0.5 * jnp.sum(weights * buoyancy, axis=0) + surface_forcing)
    center = 5.0 + 2.0 / (1.0 + jnp.sum(weights, axis=0))
    ocean_pad = jnp.pad(ocean, 1)

    def operate(values):
        return barotropic(jnp.pad(values, 1), ocean_pad, center)

    pressure = initial_pressure
    residual = forcing - operate(pressure)
    direction = residual
    norm_now = jnp.sum(residual * residual)
    for iteration in range(ITERS):
        mapped = operate(direction)
        step_size = norm_now / jnp.sum(direction * mapped)
        pressure = pressure + step_size * direction
        residual = residual - step_size * mapped
        norm_next = jnp.sum(residual * residual)
        direction = residual + (norm_next / norm_now) * direction
        norm_now = norm_next
    gradient = slope(jnp.pad(pressure, 1), ocean_pad)
    return new_tracers, pressure, gradient
```

```python
import functools

import jax
import jax.numpy as jnp
from jax import lax
from jax.experimental import pallas as pl
from jax.experimental.pallas import tpu as pltpu
from jax.sharding import PartitionSpec as P

ITERS = 4
F32 = jnp.float32
AXES = ("gx", "gy")
MIB = 1024 * 1024


def roll(values, shift, axis):
    size = values.shape[axis]
    if isinstance(shift, int):
        shift = shift % size
        if shift == 0:
            return values
    return pltpu.roll(values, shift, axis)


def lanes(shape):
    return lax.broadcasted_iota(jnp.int32, shape, len(shape) - 1)


def rows(shape):
    return lax.broadcasted_iota(jnp.int32, shape, len(shape) - 2)


def pack_columns(load, levels):
    half = levels // 2
    groups = []
    for group in range(2):
        packed = None
        for at in range(half):
            values = load(group * half + at)
            moved = roll(values, 4 * at - 126, 1)
            if packed is None:
                packed = moved
            else:
                packed = jnp.where(lanes(moved.shape) // 4 == at, moved, packed)
        groups.append(packed)
    low = lanes(groups[0].shape) % 4 < 2
    last = jnp.where(low, groups[0], roll(groups[1], 2, 1))
    first = jnp.where(low, roll(groups[0], -2, 1), groups[1])
    return last, first


def unpack_groups(from_west, from_east):
    low = lanes(from_west.shape) % 4 < 2
    return (
        jnp.where(low, from_west, roll(from_east, 2, 1)),
        jnp.where(low, roll(from_west, -2, 1), from_east),
    )


def pack_buoyancy_kernel(tracers_ref, counts_ref, b_ref, east_ref, west_ref, north_ref, south_ref):
    levels, height = b_ref.shape[0], b_ref.shape[1]
    counts = counts_ref[...].astype(F32)

    def load(level):
        values = 0.2 * tracers_ref[0, level] - 0.8 * tracers_ref[1, level]
        b_ref[level] = values
        north_ref[2 * level : 2 * level + 2, :] = values[height - 2 : height, :]
        south_ref[8 + 2 * level : 10 + 2 * level, :] = values[0:2, :]
        return values

    last, first = pack_columns(load, levels)
    east_ref[0] = last
    west_ref[0] = first
    east_ref[1] = counts
    west_ref[1] = counts
    north_ref[2 * levels : 2 * levels + 8, :] = counts[height - 8 : height, :]
    south_ref[0:8, :] = counts[0:8, :]


def pack_tracers_kernel(tracers_ref, east_ref, west_ref, north_ref, south_ref):
    levels, height = tracers_ref.shape[1], tracers_ref.shape[2]

    def load(level):
        north_ref[0, 2 * level : 2 * level + 2, :] = tracers_ref[0, level, height - 2 : height, :]
        south_ref[0, 2 * level : 2 * level + 2, :] = tracers_ref[0, level, 0:2, :]
        return tracers_ref[0, level]

    last, first = pack_columns(load, levels)
    east_ref[0] = last
    west_ref[0] = first


def weights_of(level, mixing, tile, masks_ref, u, v):
    u8, u1 = u * (8.0 / 12.0), u * (1.0 / 12.0)
    v8, v1 = v * (8.0 / 12.0), v * (1.0 / 12.0)
    plain = (mixing - u8, mixing + u8, u1, -u1, mixing - v8, mixing + v8, v1, -v1)
    height = level.astype(F32)
    out = [jnp.where(height < masks_ref[at, tile, :], plain[at], 0.0) for at in range(8)]
    total = out[0]
    for weight in out[1:]:
        total = total + weight
    return out, 1.0 - total


def stencil(weights, own, tile_at, tiles, load_at, side, north_1, north_2, south_1, south_2):
    column = lanes(own.shape)
    row = rows(own.shape)
    base = 8 * tile_at
    width = own.shape[1]
    if tile_at + 1 < tiles:
        n1, n2 = load_at(base + 1), load_at(base + 2)
    else:
        n1 = jnp.where(row == 7, north_1(), roll(own, -1, 0))
        n2 = jnp.where(row >= 6, north_2(), roll(own, -2, 0))
    if tile_at > 0:
        s1, s2 = load_at(base - 1), load_at(base - 2)
    else:
        s1 = jnp.where(row == 0, south_1(), roll(own, 1, 0))
        s2 = jnp.where(row < 2, south_2(), roll(own, 2, 0))
    near, middle = weights
    total = middle * own
    for weight, value in zip(
        near,
        (
            roll(jnp.where(column < 1, side, own), -1, 1),
            roll(jnp.where(column >= width - 1, side, own), 1, 1),
            roll(jnp.where(column < 2, side, own), -2, 1),
            roll(jnp.where(column >= width - 2, side, own), 2, 1),
            n1,
            s1,
            n2,
            s2,
        ),
    ):
        total = total + weight * value
    return total


def forcing_kernel(
    b_ref,
    counts_ref,
    u_ref,
    v_ref,
    depth_ref,
    lat_ref,
    thick_ref,
    surface_ref,
    pressure_ref,
    from_west_ref,
    from_east_ref,
    from_north_ref,
    from_south_ref,
    fields_ref,
    masks_ref,
    counts_s,
    groups_s,
    sides_s,
):
    step, steps = pl.program_id(0), pl.num_programs(0)
    chunk, height, width = b_ref.shape
    levels = chunk * steps
    tiles = height // 8

    @pl.when(step == 0)
    def _():
        gx, gy = lax.axis_index("gx"), lax.axis_index("gy")
        end_x, end_y = lax.axis_size("gx") - 1, lax.axis_size("gy") - 1
        counts = counts_ref[...].astype(F32)
        column = lanes(counts.shape)
        west = from_west_ref[1] * jnp.where(gx > 0, 1.0, 0.0)
        east = from_east_ref[1] * jnp.where(gx < end_x, 1.0, 0.0)
        masks_ref[0] = jnp.minimum(counts, roll(jnp.where(column < 1, east, counts), -1, 1))
        masks_ref[1] = jnp.minimum(counts, roll(jnp.where(column >= width - 1, west, counts), 1, 1))
        masks_ref[2] = jnp.minimum(counts, roll(jnp.where(column < 2, east, counts), -2, 1))
        masks_ref[3] = jnp.minimum(counts, roll(jnp.where(column >= width - 2, west, counts), 2, 1))
        counts_s[0:8, :] = from_south_ref[96:104, :] * jnp.where(gy > 0, 1.0, 0.0)
        counts_s[8 : 8 + height, :] = counts
        counts_s[8 + height : 16 + height, :] = from_north_ref[0:8, :] * jnp.where(gy < end_y, 1.0, 0.0)
        masks_ref[4] = jnp.minimum(counts, counts_s[9 : 9 + height, :])
        masks_ref[5] = jnp.minimum(counts, counts_s[7 : 7 + height, :])
        masks_ref[6] = jnp.minimum(counts, counts_s[10 : 10 + height, :])
        masks_ref[7] = jnp.minimum(counts, counts_s[6 : 6 + height, :])
        row = rows(counts.shape)
        lat = jnp.zeros(counts.shape, F32)
        for at in range(height):
            lat = jnp.where(row == at, lat_ref[at], lat)
        masks_ref[8] = lat
        groups_s[0], groups_s[1] = unpack_groups(from_west_ref[0], from_east_ref[0])
        fields_ref[0] = jnp.zeros((height, width), F32)
        fields_ref[1] = pressure_ref[...]
        fields_ref[2] = jnp.zeros((height, width), F32)

    group = step * chunk // 24
    for at in range(chunk):
        sides_s[at] = pltpu.roll(groups_s[group], 126 - 4 * (step * chunk + at - 24 * group), 1)

    def level_body(at, carry):
        level = step * chunk + at
        thick = thick_ref[level]
        forcing, depth_sum = list(carry[0]), list(carry[1])
        for tile_at in range(tiles):
            tile = pl.ds(8 * tile_at, 8)
            mixing = depth_ref[level] * masks_ref[8, tile, :]
            weights = weights_of(level, mixing, tile, masks_ref, u_ref[at, tile, :], v_ref[at, tile, :])
            value = stencil(
                weights,
                b_ref[at, tile, :],
                tile_at,
                tiles,
                lambda start: b_ref[at, pl.ds(start, 8), :],
                sides_s[at, tile, :],
                lambda: from_north_ref[pl.ds(2 * level + 1, 8), :],
                lambda: from_north_ref[pl.ds(2 * level + 2, 8), :],
                lambda: from_south_ref[pl.ds(2 * level + 1, 8), :],
                lambda: from_south_ref[pl.ds(2 * level, 8), :],
            )
            weight = jnp.where(level.astype(F32) < counts_s[pl.ds(8 + 8 * tile_at, 8), :], thick, 0.0)
            forcing[tile_at] = forcing[tile_at] + weight * value
            depth_sum[tile_at] = depth_sum[tile_at] + weight
        return tuple(forcing), tuple(depth_sum)

    start = (
        tuple(fields_ref[0, pl.ds(8 * at, 8), :] for at in range(tiles)),
        tuple(fields_ref[2, pl.ds(8 * at, 8), :] for at in range(tiles)),
    )
    forcing, depth_sum = lax.fori_loop(0, chunk, level_body, start)
    for at in range(tiles):
        fields_ref[0, pl.ds(8 * at, 8), :] = forcing[at]
        fields_ref[2, pl.ds(8 * at, 8), :] = depth_sum[at]

    @pl.when(step == steps - 1)
    def _():
        ocean = jnp.where(counts_s[8 : 8 + height, :] > 0.0, 1.0, 0.0)
        fields_ref[0] = ocean * (0.5 * fields_ref[0] + surface_ref[...])
        fields_ref[2] = 5.0 + 2.0 / (1.0 + fields_ref[2])


def advance_kernel(
    tracers_ref,
    u_ref,
    v_ref,
    depth_ref,
    masks_ref,
    from_west_ref,
    from_east_ref,
    from_north_ref,
    from_south_ref,
    out_ref,
    groups_s,
    north_s,
    south_s,
    sides_s,
):
    step = pl.program_id(0)
    kinds, chunk, height, width = tracers_ref.shape
    tiles = height // 8
    levels = from_north_ref.shape[1] // 2

    @pl.when(step == 0)
    def _():
        for kind in range(kinds):
            groups_s[kind, 0], groups_s[kind, 1] = unpack_groups(from_west_ref[kind], from_east_ref[kind])
            north_s[8 + 2 * levels * kind : 8 + 2 * levels * (kind + 1), :] = from_north_ref[kind]
            south_s[2 * levels * kind : 2 * levels * (kind + 1), :] = from_south_ref[kind]
        north_s[0:8, :] = jnp.zeros((8, width), F32)
        south_s[2 * levels * kinds : 2 * levels * kinds + 8, :] = jnp.zeros((8, width), F32)

    def level_body(at, carry):
        level = step * chunk + at
        group = level // 24
        shift = 126 - 4 * (level - 24 * group)
        for kind in range(kinds):
            sides_s[kind] = pltpu.roll(groups_s[kind, group], shift, 1)
        for tile_at in range(tiles):
            tile = pl.ds(8 * tile_at, 8)
            mixing = depth_ref[level] * masks_ref[8, tile, :]
            weights = weights_of(level, mixing, tile, masks_ref, u_ref[at, tile, :], v_ref[at, tile, :])
            for kind in range(kinds):
                place = 2 * (levels * kind + level)
                out_ref[kind, at, tile, :] = stencil(
                    weights,
                    tracers_ref[kind, at, tile, :],
                    tile_at,
                    tiles,
                    lambda start: tracers_ref[kind, at, pl.ds(start, 8), :],
                    sides_s[kind, tile, :],
                    lambda: north_s[pl.ds(place + 1, 8), :],
                    lambda: north_s[pl.ds(place + 2, 8), :],
                    lambda: south_s[pl.ds(place + 1, 8), :],
                    lambda: south_s[pl.ds(place, 8), :],
                )
        return carry

    lax.fori_loop(0, chunk, level_body, 0)


def outer_rows_kernel(fields_ref, from_west_ref, from_east_ref, side_ref, north_ref, south_ref):
    count, height, width = fields_ref.shape
    for at in range(count):
        side = jnp.where(lanes((height, width)) < width // 2, from_east_ref[at], from_west_ref[at])
        side_ref[at] = side
        north_ref[at] = fields_ref[at, height - 8 : height, :]
        north_ref[count + at] = side[height - 8 : height, :]
        south_ref[at] = fields_ref[at, 0:8, :]
        south_ref[count + at] = side[0:8, :]


def extended(fields_ref, side_ref, from_north_ref, from_south_ref, at):
    count = fields_ref.shape[0]
    own = jnp.concatenate([fields_ref[at], from_north_ref[at], from_south_ref[at]], axis=0)
    side = jnp.concatenate([side_ref[at], from_north_ref[count + at], from_south_ref[count + at]], axis=0)
    return jnp.concatenate([own, side], axis=1)


def krylov_kernel(fields_ref, side_ref, from_north_ref, from_south_ref, basis_ref, sums_ref):
    height, width = fields_ref.shape[1], fields_ref.shape[2]
    forcing, pressure, center = (
        extended(fields_ref, side_ref, from_north_ref, from_south_ref, at) for at in range(3)
    )
    shape = forcing.shape
    column, row = lanes(shape), rows(shape)
    gx, gy = lax.axis_index("gx"), lax.axis_index("gy")
    end_x, end_y = lax.axis_size("gx") - 1, lax.axis_size("gy") - 1
    least_column = jnp.where(gx < end_x, 0, width)
    most_column = jnp.where(gx > 0, 2 * width, width + width // 2)
    least_row = jnp.where(gy < end_y, 0, height)
    most_row = jnp.where(gy > 0, height + 16, height + 8)
    inside_x = (column < width) | ((column >= least_column) & (column < width + width // 2) & (gx < end_x)) | (
        (column >= width + width // 2) & (column < most_column)
    )
    inside_y = (row < height) | ((row >= least_row) & (row < height + 8) & (gy < end_y)) | (
        (row >= height + 8) & (row < most_row)
    )
    ocean = jnp.where((center < 6.75) & inside_x & inside_y, 1.0, 0.0)
    diagonal = jnp.where(ocean > 0.0, center, 1.0)

    def operate(values):
        seen = ocean * values
        beside = roll(seen, 1, 1) + roll(seen, -1, 1)
        mixed = seen + 0.25 * beside
        return diagonal * values - ocean * (beside + (roll(mixed, 1, 0) + roll(mixed, -1, 0)))

    def scaled(values):
        return 0.2 * operate(values) - values

    base = [forcing - operate(pressure)]
    base.append(scaled(base[0]))
    base.append(2.0 * scaled(base[1]) - base[0])
    base.append(2.0 * scaled(base[2]) - base[1])
    last = scaled(base[3])
    for at in range(4):
        basis_ref[at] = base[at]
    basis_ref[4] = pressure
    basis_ref[5] = ocean
    inner = [values[0:height, 0:width] for values in base]
    sums = []
    for at in range(4):
        for other in range(at + 1):
            sums.append(inner[at] * inner[other])
    sums.append(inner[3] * last[0:height, 0:width])
    line = jnp.zeros((8, width), F32)
    for at, values in enumerate(sums):
        part = values[0:8]
        for start in range(8, height, 8):
            part = part + values[start : start + 8]
        total = jnp.sum(jnp.sum(part, axis=0, keepdims=True), axis=1, keepdims=True)
        line = jnp.where(lanes(line.shape) == at, total, line)
    for start in range(0, sums_ref.shape[0], 8):
        sums_ref[start : start + 8, :] = line


def finish_kernel(basis_ref, sums_ref, pressure_ref, gradient_ref):
    height, width = pressure_ref.shape
    part = sums_ref[0:8, :]
    for start in range(8, sums_ref.shape[0], 8):
        part = part + sums_ref[start : start + 8, :]
    line = jnp.sum(part, axis=0, keepdims=True)

    def entry(at):
        return jnp.sum(jnp.where(lanes(line.shape) == at, line, 0.0), axis=1, keepdims=True)

    gram = [[None] * 4 for _ in range(4)]
    at = 0
    for i in range(4):
        for j in range(i + 1):
            gram[i][j] = gram[j][i] = entry(at)
            at += 1
    tail = entry(at)

    def scaled(coef):
        out = [None] * 5
        for j, value in enumerate(coef):
            if value is None:
                continue
            moves = [(1, value)] if j == 0 else [(j + 1, 0.5 * value), (j - 1, 0.5 * value)]
            for place, amount in moves:
                out[place] = amount if out[place] is None else out[place] + amount
        return out

    def dot(left, right):
        total = None
        for i in range(4):
            for j in range(4):
                if left[i] is None or right[j] is None:
                    continue
                term = left[i] * right[j] * gram[i][j]
                total = term if total is None else total + term
        return total

    def plus(left, factor, right):
        out = []
        for a, b in zip(left, right):
            if b is None:
                out.append(a)
            elif a is None:
                out.append(factor * b)
            else:
                out.append(a + factor * b)
        return out

    one = jnp.ones_like(tail)
    residual = [one, None, None, None]
    direction = [one, None, None, None]
    solution_coef = [None] * 4
    norm = dot(residual, residual)
    for step in range(ITERS):
        moved = scaled(direction)
        if step < ITERS - 1:
            energy = dot(direction, moved[:4])
        else:
            low = direction[:3] + [None]
            moved_low = scaled(low)[:4]
            energy = (
                dot(low, moved_low)
                + 2.0 * direction[3] * dot([None, None, None, one], moved_low)
                + direction[3] * direction[3] * tail
            )
        energy = 5.0 * (energy + dot(direction, direction))
        factor = norm / energy
        solution_coef = plus(solution_coef, factor, direction)
        if step < ITERS - 1:
            image = plus([None if m is None else 5.0 * m for m in moved[:4]], 5.0, direction)
            residual = plus(residual, -factor, image)
            new = dot(residual, residual)
            direction = plus(residual, new / norm, direction)
            norm = new

    pressure = basis_ref[4]
    for j in range(4):
        pressure = pressure + solution_coef[j] * basis_ref[j]
    ocean = basis_ref[5]
    seen = ocean * pressure
    half = 0.5 * ocean
    east = half * (roll(seen, -1, 1) - roll(seen, 1, 1))
    north = half * (roll(seen, -1, 0) - roll(seen, 1, 0))
    pressure_ref[...] = pressure[0:height, 0:width]
    gradient_ref[0] = east[0:height, 0:width]
    gradient_ref[1] = north[0:height, 0:width]


def shifted(values, axis, by):
    count = lax.axis_size(axis)
    return lax.ppermute(values, axis, [(i, (i + by) % count) for i in range(count)])


def full(shape):
    return pl.BlockSpec(shape, lambda *_: (0,) * len(shape))


def smem():
    return pl.BlockSpec(memory_space=pltpu.SMEM)


def params(limit=32, **more):
    return pltpu.CompilerParams(vmem_limit_bytes=limit * MIB, **more)


def struct(*shape):
    return jax.ShapeDtypeStruct(shape, F32)


def per_device(
    tracers,
    level_counts,
    u_vel,
    v_vel,
    diff_depth,
    diff_lat,
    thickness,
    surface_forcing,
    initial_pressure,
):
    kinds, levels, height, width = tracers.shape
    packed = 2 * levels
    chunk = 8
    with jax.named_scope("pack_buoyancy"):
        buoyancy, east, west, north, south = pl.pallas_call(
            pack_buoyancy_kernel,
            grid=(1,),
            in_specs=[
                pl.BlockSpec((2, levels, height, width), lambda i: (0, 0, 0, 0)),
                full((height, width)),
            ],
            out_specs=[
                full((levels, height, width)),
                full((2, height, width)),
                full((2, height, width)),
                full((packed + 8, width)),
                full((packed + 8, width)),
            ],
            out_shape=[
                struct(levels, height, width),
                struct(2, height, width),
                struct(2, height, width),
                struct(packed + 8, width),
                struct(packed + 8, width),
            ],
            compiler_params=params(),
        )(tracers, level_counts)
    with jax.named_scope("buoyancy_halo"):
        from_west = shifted(east, "gx", 1)
        from_east = shifted(west, "gx", -1)
        from_south = shifted(north, "gy", 1)
        from_north = shifted(south, "gy", -1)
    with jax.named_scope("pack_tracers"):
        t_east, t_west, t_north, t_south = pl.pallas_call(
            pack_tracers_kernel,
            grid=(kinds,),
            in_specs=[pl.BlockSpec((1, levels, height, width), lambda i: (i, 0, 0, 0))],
            out_specs=[
                pl.BlockSpec((1, height, width), lambda i: (i, 0, 0)),
                pl.BlockSpec((1, height, width), lambda i: (i, 0, 0)),
                pl.BlockSpec((1, packed, width), lambda i: (i, 0, 0)),
                pl.BlockSpec((1, packed, width), lambda i: (i, 0, 0)),
            ],
            out_shape=[
                struct(kinds, height, width),
                struct(kinds, height, width),
                struct(kinds, packed, width),
                struct(kinds, packed, width),
            ],
            compiler_params=params(56),
            cost_estimate=pl.CostEstimate(flops=20_000_000, bytes_accessed=11_000_000, transcendentals=0),
        )(tracers)
    with jax.named_scope("forcing"):
        fields, masks = pl.pallas_call(
            forcing_kernel,
            grid=(levels // chunk,),
            in_specs=[
                pl.BlockSpec((chunk, height, width), lambda i: (i, 0, 0)),
                full((height, width)),
                pl.BlockSpec((chunk, height, width), lambda i: (i, 0, 0)),
                pl.BlockSpec((chunk, height, width), lambda i: (i, 0, 0)),
                smem(),
                smem(),
                smem(),
                full((height, width)),
                full((height, width)),
                full((2, height, width)),
                full((2, height, width)),
                full((packed + 8, width)),
                full((packed + 8, width)),
            ],
            out_specs=[full((3, height, width)), full((9, height, width))],
            out_shape=[struct(3, height, width), struct(9, height, width)],
            scratch_shapes=[
                pltpu.VMEM((height + 16, width), F32),
                pltpu.VMEM((2, height, width), F32),
                pltpu.VMEM((chunk, height, width), F32),
            ],
            compiler_params=params(),
        )(
            buoyancy,
            level_counts,
            u_vel,
            v_vel,
            diff_depth,
            diff_lat,
            thickness,
            surface_forcing,
            initial_pressure,
            from_west,
            from_east,
            from_north,
            from_south,
        )
    with jax.named_scope("fields_halo"):
        f_west = shifted(fields, "gx", 1)
        f_east = shifted(fields, "gx", -1)
        side, f_north, f_south = pl.pallas_call(
            outer_rows_kernel,
            out_shape=[struct(3, height, width), struct(6, 8, width), struct(6, 8, width)],
        )(fields, f_west, f_east)
        g_south = shifted(f_north, "gy", 1)
        g_north = shifted(f_south, "gy", -1)
    with jax.named_scope("tracer_halo"):
        t_from_west = shifted(t_east, "gx", 1)
        t_from_east = shifted(t_west, "gx", -1)
        t_from_south = shifted(t_north, "gy", 1)
        t_from_north = shifted(t_south, "gy", -1)
    with jax.named_scope("krylov"):
        basis, sums = pl.pallas_call(
            krylov_kernel,
            out_shape=[struct(6, height + 16, 2 * width), struct(128, width)],
            compiler_params=params(),
        )(fields, side, g_north, g_south)
        all_sums = lax.all_to_all(sums, AXES, 0, 0, tiled=True)
        pressure, gradient = pl.pallas_call(
            finish_kernel,
            out_shape=[struct(height, width), struct(2, height, width)],
            compiler_params=params(),
        )(basis, all_sums)
    chunk = 4
    with jax.named_scope("advance"):
        new_tracers = pl.pallas_call(
            advance_kernel,
            grid=(levels // chunk,),
            in_specs=[
                pl.BlockSpec((kinds, chunk, height, width), lambda i: (0, i, 0, 0)),
                pl.BlockSpec((chunk, height, width), lambda i: (i, 0, 0)),
                pl.BlockSpec((chunk, height, width), lambda i: (i, 0, 0)),
                smem(),
                full((9, height, width)),
                full((kinds, height, width)),
                full((kinds, height, width)),
                full((kinds, packed, width)),
                full((kinds, packed, width)),
            ],
            out_specs=pl.BlockSpec((kinds, chunk, height, width), lambda i: (0, i, 0, 0)),
            out_shape=struct(kinds, levels, height, width),
            scratch_shapes=[
                pltpu.VMEM((kinds, 2, height, width), F32),
                pltpu.VMEM((kinds * packed + 8, width), F32),
                pltpu.VMEM((kinds * packed + 8, width), F32),
                pltpu.VMEM((kinds, height, width), F32),
            ],
            compiler_params=params(56),
            cost_estimate=pl.CostEstimate(flops=60_000_000, bytes_accessed=22_000_000, transcendentals=0),
        )(tracers, u_vel, v_vel, diff_depth, masks, t_from_west, t_from_east, t_from_north, t_from_south)
    return new_tracers, pressure, gradient


def solution(mesh):
    return jax.shard_map(
        per_device,
        mesh=mesh,
        in_specs=(
            P(None, None, "gy", "gx"),
            P("gy", "gx"),
            P(None, "gy", "gx"),
            P(None, "gy", "gx"),
            P(),
            P("gy"),
            P(),
            P("gy", "gx"),
            P("gy", "gx"),
        ),
        out_specs=(P(None, None, "gy", "gx"), P("gy", "gx"), P(None, "gy", "gx")),
        check_vma=False,
    )
```

```python
import functools

import jax
import jax.numpy as jnp
from jax import lax
from jax.experimental import pallas as pl
from jax.experimental.pallas import tpu as pltpu
from jax.sharding import PartitionSpec as P

ITERS = 4
F32 = jnp.float32
AXES = ("gx", "gy")
MIB = 1024 * 1024


def roll(values, shift, axis):
    size = values.shape[axis]
    if isinstance(shift, int):
        shift = shift % size
        if shift == 0:
            return values
    return pltpu.roll(values, shift, axis)


def lanes(shape):
    return lax.broadcasted_iota(jnp.int32, shape, len(shape) - 1)


def rows(shape):
    return lax.broadcasted_iota(jnp.int32, shape, len(shape) - 2)


def pack_columns(load, levels):
    half = levels // 2
    groups = []
    for group in range(2):
        packed = None
        for at in range(half):
            values = load(group * half + at)
            moved = roll(values, 4 * at - 126, 1)
            if packed is None:
                packed = moved
            else:
                packed = jnp.where(lanes(moved.shape) // 4 == at, moved, packed)
        groups.append(packed)
    low = lanes(groups[0].shape) % 4 < 2
    last = jnp.where(low, groups[0], roll(groups[1], 2, 1))
    first = jnp.where(low, roll(groups[0], -2, 1), groups[1])
    return last, first


def unpack_groups(from_west, from_east):
    low = lanes(from_west.shape) % 4 < 2
    return (
        jnp.where(low, from_west, roll(from_east, 2, 1)),
        jnp.where(low, roll(from_west, -2, 1), from_east),
    )


def is_even(axis):
    return lax.axis_index(axis) % 2 == 0


def copy_in(source, place, semaphore, parts):
    copies = []
    size = source.shape[0] // parts
    for part in range(parts):
        where = pl.ds(part * size, size)
        copies.append(pltpu.make_async_copy(source.at[where], place.at[where], semaphore.at[part]))
        copies[-1].start()
    return copies


def pack_buoyancy_kernel(
    tracers_ref, counts_ref, b_ref, x_first_ref, x_second_ref, y_first_ref, y_second_ref, held, semaphore
):
    levels, height = b_ref.shape[0], b_ref.shape[1]
    parts = semaphore.shape[0] // 2
    warm = copy_in(tracers_ref.at[0], held.at[0], semaphore.at[pl.ds(0, parts)], parts)
    salt = copy_in(tracers_ref.at[1], held.at[1], semaphore.at[pl.ds(parts, parts)], parts)
    counts = counts_ref[...].astype(F32)
    even_x, even_y = is_even("gx"), is_even("gy")

    def load(level):
        if level % (levels // parts) == 0:
            warm[level // (levels // parts)].wait()
            salt[level // (levels // parts)].wait()
        values = 0.2 * held[0, level] - 0.8 * held[1, level]
        b_ref[level] = values
        high, low = values[height - 2 : height, :], values[0:2, :]
        y_first_ref[8 + 2 * level : 10 + 2 * level, :] = jnp.where(even_y, high, low)
        y_second_ref[8 + 2 * level : 10 + 2 * level, :] = jnp.where(even_y, low, high)
        return values

    last, first = pack_columns(load, levels)
    x_first_ref[0] = jnp.where(even_x, last, first)
    x_second_ref[0] = jnp.where(even_x, first, last)
    x_first_ref[1] = counts
    x_second_ref[1] = counts
    low, high = counts[0:8, :], counts[height - 8 : height, :]
    for start in (0, 8 + 2 * levels):
        y_first_ref[start : start + 8, :] = jnp.where(even_y, high, low)
        y_second_ref[start : start + 8, :] = jnp.where(even_y, low, high)


def pack_tracers_kernel(tracers_ref, x_first_ref, x_second_ref, y_first_ref, y_second_ref, held, semaphore):
    kinds, levels, height, width = tracers_ref.shape
    even_x, even_y = is_even("gx"), is_even("gy")
    for kind in range(kinds):
        pltpu.make_async_copy(tracers_ref.at[kind], held.at[kind], semaphore.at[kind]).start()

    def one_kind(kind, carry):
        pltpu.make_async_copy(tracers_ref.at[kind], held.at[kind], semaphore.at[kind]).wait()

        def load(level):
            high, low = held[kind, level, height - 2 : height, :], held[kind, level, 0:2, :]
            y_first_ref[kind, 2 * level : 2 * level + 2, :] = jnp.where(even_y, high, low)
            y_second_ref[kind, 2 * level : 2 * level + 2, :] = jnp.where(even_y, low, high)
            return held[kind, level]

        last, first = pack_columns(load, levels)
        x_first_ref[kind] = jnp.where(even_x, last, first)
        x_second_ref[kind] = jnp.where(even_x, first, last)
        return carry

    lax.fori_loop(0, kinds, one_kind, 0)


def weights_of(level, mixing, tile, masks_ref, u, v):
    u8, u1 = u * (8.0 / 12.0), u * (1.0 / 12.0)
    v8, v1 = v * (8.0 / 12.0), v * (1.0 / 12.0)
    plain = (mixing - u8, mixing + u8, u1, -u1, mixing - v8, mixing + v8, v1, -v1)
    height = level.astype(F32)
    out = [jnp.where(height < masks_ref[at, tile, :], plain[at], 0.0) for at in range(8)]
    total = out[0]
    for weight in out[1:]:
        total = total + weight
    return out, 1.0 - total


def stencil(weights, own, tile_at, tiles, load_at, side, north_1, north_2, south_1, south_2):
    column = lanes(own.shape)
    row = rows(own.shape)
    base = 8 * tile_at
    width = own.shape[1]
    if tile_at + 1 < tiles:
        n1, n2 = load_at(base + 1), load_at(base + 2)
    else:
        n1 = jnp.where(row == 7, north_1(), roll(own, -1, 0))
        n2 = jnp.where(row >= 6, north_2(), roll(own, -2, 0))
    if tile_at > 0:
        s1, s2 = load_at(base - 1), load_at(base - 2)
    else:
        s1 = jnp.where(row == 0, south_1(), roll(own, 1, 0))
        s2 = jnp.where(row < 2, south_2(), roll(own, 2, 0))
    near, middle = weights
    total = middle * own
    for weight, value in zip(
        near,
        (
            roll(jnp.where(column < 1, side, own), -1, 1),
            roll(jnp.where(column >= width - 1, side, own), 1, 1),
            roll(jnp.where(column < 2, side, own), -2, 1),
            roll(jnp.where(column >= width - 2, side, own), 2, 1),
            n1,
            s1,
            n2,
            s2,
        ),
    ):
        total = total + weight * value
    return total


def forcing_kernel(
    b_ref,
    counts_ref,
    u_ref,
    v_ref,
    depth_ref,
    lat_ref,
    thick_ref,
    surface_ref,
    pressure_ref,
    x_first_ref,
    x_second_ref,
    y_first_ref,
    y_second_ref,
    fields_ref,
    masks_ref,
    counts_s,
    sides_s,
    north_s,
    south_s,
):
    levels, height, width = b_ref.shape
    tiles = height // 8
    half = levels // 2
    gx, gy = lax.axis_index("gx"), lax.axis_index("gy")
    even_x, even_y = is_even("gx"), is_even("gy")
    end_x, end_y = lax.axis_size("gx") - 1, lax.axis_size("gy") - 1
    counts = counts_ref[...].astype(F32)
    column = lanes(counts.shape)
    east = jnp.where(even_x, x_first_ref[1], x_second_ref[1]) * jnp.where(gx < end_x, 1.0, 0.0)
    west = jnp.where(even_x, x_second_ref[1], x_first_ref[1]) * jnp.where(gx > 0, 1.0, 0.0)
    north_s[...] = jnp.where(even_y, y_first_ref[...], y_second_ref[...])
    south_s[...] = jnp.where(even_y, y_second_ref[...], y_first_ref[...])
    masks_ref[0] = jnp.minimum(counts, roll(jnp.where(column < 1, east, counts), -1, 1))
    masks_ref[1] = jnp.minimum(counts, roll(jnp.where(column >= width - 1, west, counts), 1, 1))
    masks_ref[2] = jnp.minimum(counts, roll(jnp.where(column < 2, east, counts), -2, 1))
    masks_ref[3] = jnp.minimum(counts, roll(jnp.where(column >= width - 2, west, counts), 2, 1))
    counts_s[0:8, :] = south_s[0:8, :] * jnp.where(gy > 0, 1.0, 0.0)
    counts_s[8 : 8 + height, :] = counts
    counts_s[8 + height : 16 + height, :] = north_s[0:8, :] * jnp.where(gy < end_y, 1.0, 0.0)
    masks_ref[4] = jnp.minimum(counts, counts_s[9 : 9 + height, :])
    masks_ref[5] = jnp.minimum(counts, counts_s[7 : 7 + height, :])
    masks_ref[6] = jnp.minimum(counts, counts_s[10 : 10 + height, :])
    masks_ref[7] = jnp.minimum(counts, counts_s[6 : 6 + height, :])
    row = rows(counts.shape)
    lat = jnp.zeros(counts.shape, F32)
    for at in range(height):
        lat = jnp.where(row == at, lat_ref[at], lat)
    masks_ref[8] = lat
    groups = unpack_groups(
        jnp.where(even_x, x_second_ref[0], x_first_ref[0]), jnp.where(even_x, x_first_ref[0], x_second_ref[0])
    )
    for level in range(levels):
        sides_s[level] = roll(groups[level // half], 126 - 4 * (level % half), 1)

    def level_body(level, carry):
        thick = thick_ref[level]
        forcing, depth_sum = list(carry[0]), list(carry[1])
        for tile_at in range(tiles):
            tile = pl.ds(8 * tile_at, 8)
            mixing = depth_ref[level] * masks_ref[8, tile, :]
            weights = weights_of(level, mixing, tile, masks_ref, u_ref[level, tile, :], v_ref[level, tile, :])
            value = stencil(
                weights,
                b_ref[level, tile, :],
                tile_at,
                tiles,
                lambda start: b_ref[level, pl.ds(start, 8), :],
                sides_s[level, tile, :],
                lambda: north_s[pl.ds(2 * level + 1, 8), :],
                lambda: north_s[pl.ds(2 * level + 2, 8), :],
                lambda: south_s[pl.ds(2 * level + 9, 8), :],
                lambda: south_s[pl.ds(2 * level + 8, 8), :],
            )
            weight = jnp.where(level.astype(F32) < counts_s[pl.ds(8 + 8 * tile_at, 8), :], thick, 0.0)
            forcing[tile_at] = forcing[tile_at] + weight * value
            depth_sum[tile_at] = depth_sum[tile_at] + weight
        return tuple(forcing), tuple(depth_sum)

    zeros = tuple(jnp.zeros((8, width), F32) for _ in range(tiles))
    forcing, depth_sum = lax.fori_loop(0, levels, level_body, (zeros, zeros), unroll=4)
    for at in range(tiles):
        tile = pl.ds(8 * at, 8)
        ocean = jnp.where(counts_s[pl.ds(8 + 8 * at, 8), :] > 0.0, 1.0, 0.0)
        fields_ref[0, tile, :] = ocean * (0.5 * forcing[at] + surface_ref[tile, :])
        fields_ref[1, tile, :] = pressure_ref[tile, :]
        fields_ref[2, tile, :] = 5.0 + 2.0 / (1.0 + depth_sum[at])


def shift_matrix():
    shape = (256, 256)
    column = lanes(shape)
    offset = rows(shape) % 128 - column % 128
    near = jnp.where(offset == 1, 1.0, 0.0)
    far = jnp.where(offset == -1, 1.0, 0.0)
    both = jnp.where(offset == 2, 1.0, 0.0) - jnp.where(offset == -2, 1.0, 0.0)
    return jnp.where(column < 128, near + far, 8.0 * (near - far) - both).astype(jnp.bfloat16)


def side_terms(sides_s, masks_ref, u_ref, depth_ref, x_first_ref, x_second_ref):
    kinds = x_first_ref.shape[0]
    levels, height, width = u_ref.shape
    half = levels // 2
    even_x = is_even("gx")
    spot = lanes((height, width)) % 4
    column = lanes((height, width))
    for group in range(2):
        near, far = jnp.zeros((height, width), F32), jnp.zeros((height, width), F32)
        for at in range(half):
            level = group * half + at
            mixing = depth_ref[level] * masks_ref[8]
            u8, u1 = u_ref[level] * (8.0 / 12.0), u_ref[level] * (1.0 / 12.0)
            first = jnp.where(
                column == width - 1,
                jnp.where(level < masks_ref[0], mixing - u8, 0.0),
                jnp.where(level < masks_ref[1], mixing + u8, 0.0),
            )
            first = jnp.where((column == 0) | (column == width - 1), first, 0.0)
            second = jnp.where(
                column < 2, jnp.where(level < masks_ref[3], -u1, 0.0), jnp.where(level < masks_ref[2], u1, 0.0)
            )
            here = column // 4 == at
            near = jnp.where(here, roll(first, 4 * at - 126, 1), near)
            far = jnp.where(here, roll(second, 4 * at - 126, 1), far)
        for kind in range(kinds):
            x_first, x_second = x_first_ref[kind], x_second_ref[kind]
            values = unpack_groups(jnp.where(even_x, x_second, x_first), jnp.where(even_x, x_first, x_second))[group]
            by_two = jnp.where(spot < 2, roll(values, -2, 1), roll(values, 2, 1))
            by_one = jnp.where(spot < 2, roll(values, -1, 1), roll(values, 1, 1))
            sides_s[kind, group] = near * by_one + far * by_two


def advance_kernel(
    tracers_ref,
    u_ref,
    v_ref,
    depth_ref,
    masks_ref,
    counts_ref,
    x_first_ref,
    x_second_ref,
    y_first_ref,
    y_second_ref,
    out_ref,
    held,
    sides_s,
    masked_s,
    parts_s,
    moved_s,
    matrix_s,
    weights_s,
    in_semaphore,
    out_semaphore,
):
    kinds, levels, height, width = tracers_ref.shape
    groups = in_semaphore.shape[0]
    chunk = levels // groups
    tiles = height // 8
    half = levels // 2

    def load(group):
        where = (slice(None), pl.ds(group * chunk, chunk))
        return pltpu.make_async_copy(tracers_ref.at[where], held.at[where], in_semaphore.at[group])

    def store(group):
        where = (slice(None), pl.ds(group * chunk, chunk))
        return pltpu.make_async_copy(held.at[where], out_ref.at[where], out_semaphore.at[group])

    for group in range(groups):
        load(group).start()
    matrix_s[...] = shift_matrix()
    side_terms(sides_s, masks_ref, u_ref, depth_ref, x_first_ref, x_second_ref)
    even_y = is_even("gy")
    column = lanes((8, width))
    outer = (column < 2) | (column >= width - 2)

    def prepare(level, at):
        number = level.astype(F32)
        for tile_at in range(tiles):
            tile = pl.ds(8 * tile_at, 8)
            mixing = depth_ref[level] * masks_ref[8, tile, :]
            u, v = u_ref[level, tile, :], v_ref[level, tile, :]
            active = number < counts_ref[pl.ds(8 + 8 * tile_at, 8), :]
            weights_s[at, 0, tile, :] = weights_of(level, mixing, tile, masks_ref, u, v)[1]
            weights_s[at, 1, tile, :] = jnp.where(active, mixing, 0.0)
            weights_s[at, 2, tile, :] = jnp.where(active, u * (-1.0 / 12.0), 0.0)
            weights_s[at, 3, tile, :] = jnp.where(active, v * (-1.0 / 12.0), 0.0)
        active = number < counts_ref[8 : 8 + height, :]
        south_active = number < counts_ref[6:8, :]
        north_active = number < counts_ref[8 + height : 10 + height, :]
        for kind in range(kinds):
            seen = jnp.where(active, held[kind, level], 0.0)
            masked_s[at, kind, 8 : 8 + height, :] = seen
            high = seen.astype(jnp.bfloat16)
            row = (at * kinds + kind) * height
            parts_s[row : row + height, 0:width] = high
            parts_s[row : row + height, width : 2 * width] = (seen - high.astype(F32)).astype(jnp.bfloat16)
            first, second = (ref[kind, pl.ds(2 * level, 2), :] for ref in (y_first_ref, y_second_ref))
            north = jnp.where(even_y, first, second)
            south = jnp.where(even_y, second, first)
            masked_s[at, kind, 8 + height : 10 + height, :] = jnp.where(north_active, north, 0.0)
            masked_s[at, kind, 6:8, :] = jnp.where(south_active, south, 0.0)

    def finish(level, at):
        group = level // half
        shift = 126 - 4 * (level - half * group)
        for tile_at in range(tiles):
            base = 8 * tile_at
            tile = pl.ds(base, 8)
            own_weight, mixing, eastward, northward = (weights_s[at, i, tile, :] for i in range(4))
            for kind in range(kinds):
                row = (at * kinds + kind) * height + base
                n1, s1, n2, s2 = (masked_s[at, kind, pl.ds(8 + base + by, 8), :] for by in (1, -1, 2, -2))
                side = jnp.where(outer, pltpu.roll(sides_s[kind, group, tile, :], shift, 1), 0.0)
                held[kind, level, tile, :] = (
                    own_weight * held[kind, level, tile, :]
                    + mixing * (moved_s[row : row + 8, 0:width] + (n1 + s1))
                    + eastward * moved_s[row : row + 8, width : 2 * width]
                    + northward * (8.0 * (n1 - s1) - (n2 - s2))
                    + side
                )

    def one_group(group, carry):
        load(group).wait()
        for at in range(chunk):
            prepare(group * chunk + at, at)
        moved_s[...] = jnp.dot(parts_s[...], matrix_s[...], preferred_element_type=F32)
        for at in range(chunk):
            finish(group * chunk + at, at)
        store(group).start()
        return carry

    lax.fori_loop(0, groups, one_group, 0)
    for group in range(groups):
        store(group).wait()


def outer_rows_kernel(fields_ref, x_first_ref, x_second_ref, side_ref, y_first_ref, y_second_ref):
    count, height, width = fields_ref.shape
    even_x, even_y = is_even("gx"), is_even("gy")
    eastern = (lanes((height, width)) < width // 2) == even_x
    for at in range(count):
        side = jnp.where(eastern, x_first_ref[at], x_second_ref[at])
        side_ref[at] = side
        for place, values in ((at, fields_ref[at]), (count + at, side)):
            low, high = values[0:8, :], values[height - 8 : height, :]
            y_first_ref[place] = jnp.where(even_y, high, low)
            y_second_ref[place] = jnp.where(even_y, low, high)


def extended(fields_ref, side_ref, y_first_ref, y_second_ref, at):
    count = fields_ref.shape[0]
    even_y = is_even("gy")

    def column(inner, place):
        first, second = y_first_ref[place], y_second_ref[place]
        return jnp.concatenate([inner, jnp.where(even_y, first, second), jnp.where(even_y, second, first)], axis=0)

    return jnp.concatenate([column(fields_ref[at], at), column(side_ref[at], count + at)], axis=1)


def krylov_kernel(fields_ref, side_ref, y_first_ref, y_second_ref, basis_ref, sums_ref):
    height, width = fields_ref.shape[1], fields_ref.shape[2]
    forcing, pressure, center = (
        extended(fields_ref, side_ref, y_first_ref, y_second_ref, at) for at in range(3)
    )
    shape = forcing.shape
    column, row = lanes(shape), rows(shape)
    gx, gy = lax.axis_index("gx"), lax.axis_index("gy")
    end_x, end_y = lax.axis_size("gx") - 1, lax.axis_size("gy") - 1
    least_column = jnp.where(gx < end_x, 0, width)
    most_column = jnp.where(gx > 0, 2 * width, width + width // 2)
    least_row = jnp.where(gy < end_y, 0, height)
    most_row = jnp.where(gy > 0, height + 16, height + 8)
    inside_x = (column < width) | ((column >= least_column) & (column < width + width // 2) & (gx < end_x)) | (
        (column >= width + width // 2) & (column < most_column)
    )
    inside_y = (row < height) | ((row >= least_row) & (row < height + 8) & (gy < end_y)) | (
        (row >= height + 8) & (row < most_row)
    )
    ocean = jnp.where((center < 6.75) & inside_x & inside_y, 1.0, 0.0)
    diagonal = jnp.where(ocean > 0.0, center, 1.0)

    def operate(values):
        seen = ocean * values
        beside = roll(seen, 1, 1) + roll(seen, -1, 1)
        mixed = seen + 0.25 * beside
        return diagonal * values - ocean * (beside + (roll(mixed, 1, 0) + roll(mixed, -1, 0)))

    def scaled(values):
        return 0.2 * operate(values) - values

    base = [forcing - operate(pressure)]
    base.append(scaled(base[0]))
    base.append(2.0 * scaled(base[1]) - base[0])
    base.append(2.0 * scaled(base[2]) - base[1])
    last = scaled(base[3])
    for at in range(4):
        basis_ref[at] = base[at]
    basis_ref[4] = pressure
    basis_ref[5] = ocean
    inner = [values[0:height, 0:width] for values in base]
    sums = []
    for at in range(4):
        for other in range(at + 1):
            sums.append(inner[at] * inner[other])
    sums.append(inner[3] * last[0:height, 0:width])
    line = jnp.zeros((8, width), F32)
    for at, values in enumerate(sums):
        part = values[0:8]
        for start in range(8, height, 8):
            part = part + values[start : start + 8]
        total = jnp.sum(jnp.sum(part, axis=0, keepdims=True), axis=1, keepdims=True)
        line = jnp.where(lanes(line.shape) == at, total, line)
    for start in range(0, sums_ref.shape[0], 8):
        sums_ref[start : start + 8, :] = line


def finish_kernel(basis_ref, sums_ref, pressure_ref, gradient_ref):
    height, width = pressure_ref.shape
    part = sums_ref[0:8, :]
    for start in range(8, sums_ref.shape[0], 8):
        part = part + sums_ref[start : start + 8, :]
    line = jnp.sum(part, axis=0, keepdims=True)

    def entry(at):
        return jnp.sum(jnp.where(lanes(line.shape) == at, line, 0.0), axis=1, keepdims=True)

    gram = [[None] * 4 for _ in range(4)]
    at = 0
    for i in range(4):
        for j in range(i + 1):
            gram[i][j] = gram[j][i] = entry(at)
            at += 1
    tail = entry(at)

    def scaled(coef):
        out = [None] * 5
        for j, value in enumerate(coef):
            if value is None:
                continue
            moves = [(1, value)] if j == 0 else [(j + 1, 0.5 * value), (j - 1, 0.5 * value)]
            for place, amount in moves:
                out[place] = amount if out[place] is None else out[place] + amount
        return out

    def dot(left, right):
        total = None
        for i in range(4):
            for j in range(4):
                if left[i] is None or right[j] is None:
                    continue
                term = left[i] * right[j] * gram[i][j]
                total = term if total is None else total + term
        return total

    def plus(left, factor, right):
        out = []
        for a, b in zip(left, right):
            if b is None:
                out.append(a)
            elif a is None:
                out.append(factor * b)
            else:
                out.append(a + factor * b)
        return out

    one = jnp.ones_like(tail)
    residual = [one, None, None, None]
    direction = [one, None, None, None]
    solution_coef = [None] * 4
    norm = dot(residual, residual)
    for step in range(ITERS):
        moved = scaled(direction)
        if step < ITERS - 1:
            energy = dot(direction, moved[:4])
        else:
            low = direction[:3] + [None]
            moved_low = scaled(low)[:4]
            energy = (
                dot(low, moved_low)
                + 2.0 * direction[3] * dot([None, None, None, one], moved_low)
                + direction[3] * direction[3] * tail
            )
        energy = 5.0 * (energy + dot(direction, direction))
        factor = norm / energy
        solution_coef = plus(solution_coef, factor, direction)
        if step < ITERS - 1:
            image = plus([None if m is None else 5.0 * m for m in moved[:4]], 5.0, direction)
            residual = plus(residual, -factor, image)
            new = dot(residual, residual)
            direction = plus(residual, new / norm, direction)
            norm = new

    pressure = basis_ref[4]
    for j in range(4):
        pressure = pressure + solution_coef[j] * basis_ref[j]
    ocean = basis_ref[5]
    seen = ocean * pressure
    half = 0.5 * ocean
    east = half * (roll(seen, -1, 1) - roll(seen, 1, 1))
    north = half * (roll(seen, -1, 0) - roll(seen, 1, 0))
    pressure_ref[...] = pressure[0:height, 0:width]
    gradient_ref[0] = east[0:height, 0:width]
    gradient_ref[1] = north[0:height, 0:width]


def exchange(first, second, axis):
    wide, tall = lax.axis_size("gx"), lax.axis_size("gy")
    pairs, others = [], []
    for x in range(wide):
        for y in range(tall):
            at = x * tall + y
            if axis == "gx":
                pairs.append((at, (x ^ 1) * tall + y))
                others.append((at, ((x + 1 if x % 2 else x - 1) % wide) * tall + y))
            else:
                pairs.append((at, x * tall + (y ^ 1)))
                beyond = y + 1 if y % 2 else y - 1
                inside = 0 <= beyond < tall
                others.append((at, x * tall + beyond if inside else (x ^ 1) * tall + y))
    return lax.ppermute(first, AXES, pairs), lax.ppermute(second, AXES, others)


def full(shape):
    return pl.BlockSpec(shape, lambda *_: (0,) * len(shape))


def vmem():
    return pl.BlockSpec(memory_space=pltpu.VMEM)


def hbm():
    return pl.BlockSpec(memory_space=pltpu.HBM)


def smem():
    return pl.BlockSpec(memory_space=pltpu.SMEM)


def params(limit=32, **more):
    return pltpu.CompilerParams(vmem_limit_bytes=limit * MIB, **more)


def struct(*shape):
    return jax.ShapeDtypeStruct(shape, F32)


def per_device(
    tracers,
    level_counts,
    u_vel,
    v_vel,
    diff_depth,
    diff_lat,
    thickness,
    surface_forcing,
    initial_pressure,
):
    kinds, levels, height, width = tracers.shape
    packed = 2 * levels
    with jax.named_scope("pack_buoyancy"):
        buoyancy, x_first, x_second, y_first, y_second = pl.pallas_call(
            pack_buoyancy_kernel,
            in_specs=[hbm(), vmem()],
            out_shape=[
                struct(levels, height, width),
                struct(2, height, width),
                struct(2, height, width),
                struct(packed + 16, width),
                struct(packed + 16, width),
            ],
            scratch_shapes=[pltpu.VMEM((2, levels, height, width), F32), pltpu.SemaphoreType.DMA((8,))],
            compiler_params=params(52),
        )(tracers, level_counts)
    with jax.named_scope("buoyancy_halo"):
        x_halo = exchange(x_first, x_second, "gx")
        y_halo = exchange(y_first, y_second, "gy")
    with jax.named_scope("pack_tracers"):
        later, _ = lax.optimization_barrier((tracers, x_first))
        t_x_first, t_x_second, t_y_first, t_y_second = pl.pallas_call(
            pack_tracers_kernel,
            in_specs=[hbm()],
            out_shape=[
                struct(kinds, height, width),
                struct(kinds, height, width),
                struct(kinds, packed, width),
                struct(kinds, packed, width),
            ],
            scratch_shapes=[pltpu.VMEM((kinds, levels, height, width), F32), pltpu.SemaphoreType.DMA((kinds,))],
            compiler_params=params(52),
            cost_estimate=pl.CostEstimate(flops=20_000_000, bytes_accessed=11_000_000, transcendentals=0),
        )(later)
        buoyancy, *tracer_packs = lax.optimization_barrier((buoyancy, t_x_first, t_x_second, t_y_first, t_y_second))
    with jax.named_scope("forcing"):
        fields, masks, counts = pl.pallas_call(
            forcing_kernel,
            in_specs=[vmem()] * 4 + [smem()] * 3 + [vmem()] * 6,
            out_shape=[struct(3, height, width), struct(9, height, width), struct(height + 16, width)],
            scratch_shapes=[
                pltpu.VMEM((levels, height, width), F32),
                pltpu.VMEM((packed + 16, width), F32),
                pltpu.VMEM((packed + 16, width), F32),
            ],
            compiler_params=params(8),
        )(
            buoyancy,
            level_counts,
            u_vel,
            v_vel,
            diff_depth,
            diff_lat,
            thickness,
            surface_forcing,
            initial_pressure,
            *x_halo,
            *y_halo,
        )
    with jax.named_scope("tracer_halo"):
        fields, t_x_first, t_x_second, t_y_first, t_y_second = lax.optimization_barrier((fields, *tracer_packs))
        t_x_halo = exchange(t_x_first, t_x_second, "gx")
        t_y_halo = exchange(t_y_first, t_y_second, "gy")
    with jax.named_scope("fields_halo"):
        f_x_halo = exchange(fields, fields, "gx")
        side, f_y_first, f_y_second = pl.pallas_call(
            outer_rows_kernel,
            out_shape=[struct(3, height, width), struct(6, 8, width), struct(6, 8, width)],
            compiler_params=params(4),
        )(fields, *f_x_halo)
        f_y_halo = exchange(f_y_first, f_y_second, "gy")
    with jax.named_scope("krylov"):
        basis, sums = pl.pallas_call(
            krylov_kernel,
            out_shape=[struct(6, height + 16, 2 * width), struct(128, width)],
            compiler_params=params(8),
        )(fields, side, *f_y_halo)
        all_sums = lax.all_to_all(sums, AXES, 0, 0, tiled=True)
        pressure, gradient = pl.pallas_call(
            finish_kernel,
            out_shape=[struct(height, width), struct(2, height, width)],
            compiler_params=params(8),
        )(basis, all_sums)
    chunk = 4
    with jax.named_scope("advance"):
        new_tracers = pl.pallas_call(
            advance_kernel,
            in_specs=[hbm(), vmem(), vmem(), smem()] + [vmem()] * 6,
            out_specs=hbm(),
            out_shape=struct(kinds, levels, height, width),
            scratch_shapes=[
                pltpu.VMEM((kinds, levels, height, width), F32),
                pltpu.VMEM((kinds, 2, height, width), F32),
                pltpu.VMEM((chunk, kinds, height + 16, width), F32),
                pltpu.VMEM((chunk * kinds * height, 2 * width), jnp.bfloat16),
                pltpu.VMEM((chunk * kinds * height, 2 * width), F32),
                pltpu.VMEM((2 * width, 2 * width), jnp.bfloat16),
                pltpu.VMEM((chunk, 4, height, width), F32),
                pltpu.SemaphoreType.DMA((levels // chunk,)),
                pltpu.SemaphoreType.DMA((levels // chunk,)),
            ],
            compiler_params=params(52),
            cost_estimate=pl.CostEstimate(flops=60_000_000, bytes_accessed=22_000_000, transcendentals=0),
        )(tracers, u_vel, v_vel, diff_depth, masks, counts, *t_x_halo, *t_y_halo)
    return new_tracers, pressure, gradient


def solution(mesh):
    return jax.shard_map(
        per_device,
        mesh=mesh,
        in_specs=(
            P(None, None, "gy", "gx"),
            P("gy", "gx"),
            P(None, "gy", "gx"),
            P(None, "gy", "gx"),
            P(),
            P("gy"),
            P(),
            P("gy", "gx"),
            P("gy", "gx"),
        ),
        out_specs=(P(None, None, "gy", "gx"), P("gy", "gx"), P(None, "gy", "gx")),
        check_vma=False,
    )
```

```python
import functools

import jax
import jax.numpy as jnp
from jax import lax
from jax.experimental import pallas as pl
from jax.experimental.pallas import tpu as pltpu
from jax.sharding import PartitionSpec as P

ITERS = 4
F32 = jnp.float32
AXES = ("gx", "gy")
MIB = 1024 * 1024


def roll(values, shift, axis):
    size = values.shape[axis]
    if isinstance(shift, int):
        shift = shift % size
        if shift == 0:
            return values
    return pltpu.roll(values, shift, axis)


def lanes(shape):
    return lax.broadcasted_iota(jnp.int32, shape, len(shape) - 1)


def rows(shape):
    return lax.broadcasted_iota(jnp.int32, shape, len(shape) - 2)


def pack_columns(load, levels):
    half = levels // 2
    groups = []
    for group in range(2):
        packed = None
        for at in range(half):
            values = load(group * half + at)
            moved = roll(values, 4 * at - 126, 1)
            if packed is None:
                packed = moved
            else:
                packed = jnp.where(lanes(moved.shape) // 4 == at, moved, packed)
        groups.append(packed)
    low = lanes(groups[0].shape) % 4 < 2
    last = jnp.where(low, groups[0], roll(groups[1], 2, 1))
    first = jnp.where(low, roll(groups[0], -2, 1), groups[1])
    return last, first


def unpack_groups(from_west, from_east):
    low = lanes(from_west.shape) % 4 < 2
    return (
        jnp.where(low, from_west, roll(from_east, 2, 1)),
        jnp.where(low, roll(from_west, -2, 1), from_east),
    )


def is_even(axis):
    return lax.axis_index(axis) % 2 == 0


def copy_in(source, place, semaphore, parts):
    copies = []
    size = source.shape[0] // parts
    for part in range(parts):
        where = pl.ds(part * size, size)
        copies.append(pltpu.make_async_copy(source.at[where], place.at[where], semaphore.at[part]))
        copies[-1].start()
    return copies


def pack_buoyancy_kernel(
    tracers_ref,
    counts_ref,
    b_ref,
    x_first_ref,
    x_second_ref,
    y_first_ref,
    y_second_ref,
    held,
    counts_s,
    semaphore,
    counts_semaphore,
):
    levels, height = b_ref.shape[0], b_ref.shape[1]
    parts = semaphore.shape[0] // 2
    warm = copy_in(tracers_ref.at[0], held.at[0], semaphore.at[pl.ds(0, parts)], parts)
    salt = copy_in(tracers_ref.at[1], held.at[1], semaphore.at[pl.ds(parts, parts)], parts)
    counts_copy = pltpu.make_async_copy(counts_ref, counts_s, counts_semaphore)
    counts_copy.start()
    even_x, even_y = is_even("gx"), is_even("gy")

    def load(level):
        if level % (levels // parts) == 0:
            warm[level // (levels // parts)].wait()
            salt[level // (levels // parts)].wait()
        values = 0.2 * held[0, level] - 0.8 * held[1, level]
        b_ref[level] = values
        high, low = values[height - 2 : height, :], values[0:2, :]
        y_first_ref[8 + 2 * level : 10 + 2 * level, :] = jnp.where(even_y, high, low)
        y_second_ref[8 + 2 * level : 10 + 2 * level, :] = jnp.where(even_y, low, high)
        return values

    last, first = pack_columns(load, levels)
    x_first_ref[0] = jnp.where(even_x, last, first)
    x_second_ref[0] = jnp.where(even_x, first, last)
    counts_copy.wait()
    counts = counts_s[...].astype(F32)
    x_first_ref[1] = counts
    x_second_ref[1] = counts
    low, high = counts[0:8, :], counts[height - 8 : height, :]
    for start in (0, 8 + 2 * levels):
        y_first_ref[start : start + 8, :] = jnp.where(even_y, high, low)
        y_second_ref[start : start + 8, :] = jnp.where(even_y, low, high)


def pack_tracers_kernel(first_kind, tracers_ref, *refs):
    x_first_ref, x_second_ref, y_first_ref, y_second_ref, held, semaphore = refs[-6:]
    kinds, levels, height, width = held.shape
    kind = pl.program_id(0)
    even_x, even_y = is_even("gx"), is_even("gy")

    @pl.when(kind == 0)
    def _():
        for at in range(kinds):
            pltpu.make_async_copy(tracers_ref.at[first_kind + at], held.at[at], semaphore.at[at]).start()

    pltpu.make_async_copy(tracers_ref.at[first_kind + kind], held.at[kind], semaphore.at[kind]).wait()

    def load(level):
        high, low = held[kind, level, height - 2 : height, :], held[kind, level, 0:2, :]
        y_first_ref[0, 2 * level : 2 * level + 2, :] = jnp.where(even_y, high, low)
        y_second_ref[0, 2 * level : 2 * level + 2, :] = jnp.where(even_y, low, high)
        return held[kind, level]

    last, first = pack_columns(load, levels)
    x_first_ref[0] = jnp.where(even_x, last, first)
    x_second_ref[0] = jnp.where(even_x, first, last)


def pack_tracers(tracers, first_kind, count, before=()):
    kinds, levels, height, width = tracers.shape
    side = pl.BlockSpec((1, height, width), lambda i: (i + first_kind, 0, 0))
    edge = pl.BlockSpec((1, 2 * levels, width), lambda i: (i + first_kind, 0, 0))
    return pl.pallas_call(
        functools.partial(pack_tracers_kernel, first_kind),
        grid=(count,),
        in_specs=[hbm()] + [pl.BlockSpec(memory_space=pl.ANY)] * len(before),
        out_specs=[side, side, edge, edge],
        out_shape=[struct(kinds, height, width)] * 2 + [struct(kinds, 2 * levels, width)] * 2,
        input_output_aliases={1 + at: at for at in range(len(before))},
        scratch_shapes=[pltpu.VMEM((count, levels, height, width), F32), pltpu.SemaphoreType.DMA((count,))],
        compiler_params=params(52),
        cost_estimate=pl.CostEstimate(flops=10_000_000, bytes_accessed=6_000_000, transcendentals=0),
    )(tracers, *before)


def weights_of(level, mixing, tile, masks_ref, u, v):
    u8, u1 = u * (8.0 / 12.0), u * (1.0 / 12.0)
    v8, v1 = v * (8.0 / 12.0), v * (1.0 / 12.0)
    plain = (mixing - u8, mixing + u8, u1, -u1, mixing - v8, mixing + v8, v1, -v1)
    height = level.astype(F32)
    out = [jnp.where(height < masks_ref[at, tile, :], plain[at], 0.0) for at in range(8)]
    total = out[0]
    for weight in out[1:]:
        total = total + weight
    return out, 1.0 - total


def stencil(weights, own, tile_at, tiles, load_at, side, north_1, north_2, south_1, south_2):
    column = lanes(own.shape)
    row = rows(own.shape)
    base = 8 * tile_at
    width = own.shape[1]
    if tile_at + 1 < tiles:
        n1, n2 = load_at(base + 1), load_at(base + 2)
    else:
        n1 = jnp.where(row == 7, north_1(), roll(own, -1, 0))
        n2 = jnp.where(row >= 6, north_2(), roll(own, -2, 0))
    if tile_at > 0:
        s1, s2 = load_at(base - 1), load_at(base - 2)
    else:
        s1 = jnp.where(row == 0, south_1(), roll(own, 1, 0))
        s2 = jnp.where(row < 2, south_2(), roll(own, 2, 0))
    near, middle = weights
    total = middle * own
    for weight, value in zip(
        near,
        (
            roll(jnp.where(column < 1, side, own), -1, 1),
            roll(jnp.where(column >= width - 1, side, own), 1, 1),
            roll(jnp.where(column < 2, side, own), -2, 1),
            roll(jnp.where(column >= width - 2, side, own), 2, 1),
            n1,
            s1,
            n2,
            s2,
        ),
    ):
        total = total + weight * value
    return total


def forcing_kernel(
    b_ref,
    counts_ref,
    u_ref,
    v_ref,
    depth_ref,
    lat_ref,
    thick_ref,
    surface_ref,
    pressure_ref,
    x_first_ref,
    x_second_ref,
    y_first_ref,
    y_second_ref,
    fields_ref,
    masks_ref,
    counts_s,
    sides_s,
    north_s,
    south_s,
):
    levels, height, width = b_ref.shape
    tiles = height // 8
    half = levels // 2
    gx, gy = lax.axis_index("gx"), lax.axis_index("gy")
    even_x, even_y = is_even("gx"), is_even("gy")
    end_x, end_y = lax.axis_size("gx") - 1, lax.axis_size("gy") - 1
    counts = counts_ref[...].astype(F32)
    column = lanes(counts.shape)
    east = jnp.where(even_x, x_first_ref[1], x_second_ref[1]) * jnp.where(gx < end_x, 1.0, 0.0)
    west = jnp.where(even_x, x_second_ref[1], x_first_ref[1]) * jnp.where(gx > 0, 1.0, 0.0)
    north_s[...] = jnp.where(even_y, y_first_ref[...], y_second_ref[...])
    south_s[...] = jnp.where(even_y, y_second_ref[...], y_first_ref[...])
    masks_ref[0] = jnp.minimum(counts, roll(jnp.where(column < 1, east, counts), -1, 1))
    masks_ref[1] = jnp.minimum(counts, roll(jnp.where(column >= width - 1, west, counts), 1, 1))
    masks_ref[2] = jnp.minimum(counts, roll(jnp.where(column < 2, east, counts), -2, 1))
    masks_ref[3] = jnp.minimum(counts, roll(jnp.where(column >= width - 2, west, counts), 2, 1))
    counts_s[0:8, :] = south_s[0:8, :] * jnp.where(gy > 0, 1.0, 0.0)
    counts_s[8 : 8 + height, :] = counts
    counts_s[8 + height : 16 + height, :] = north_s[0:8, :] * jnp.where(gy < end_y, 1.0, 0.0)
    masks_ref[4] = jnp.minimum(counts, counts_s[9 : 9 + height, :])
    masks_ref[5] = jnp.minimum(counts, counts_s[7 : 7 + height, :])
    masks_ref[6] = jnp.minimum(counts, counts_s[10 : 10 + height, :])
    masks_ref[7] = jnp.minimum(counts, counts_s[6 : 6 + height, :])
    row = rows(counts.shape)
    lat = jnp.zeros(counts.shape, F32)
    for at in range(height):
        lat = jnp.where(row == at, lat_ref[at], lat)
    masks_ref[8] = lat
    groups = unpack_groups(
        jnp.where(even_x, x_second_ref[0], x_first_ref[0]), jnp.where(even_x, x_first_ref[0], x_second_ref[0])
    )
    for level in range(levels):
        sides_s[level] = roll(groups[level // half], 126 - 4 * (level % half), 1)

    def level_body(level, carry):
        thick = thick_ref[level]
        forcing, depth_sum = list(carry[0]), list(carry[1])
        for tile_at in range(tiles):
            tile = pl.ds(8 * tile_at, 8)
            mixing = depth_ref[level] * masks_ref[8, tile, :]
            weights = weights_of(level, mixing, tile, masks_ref, u_ref[level, tile, :], v_ref[level, tile, :])
            value = stencil(
                weights,
                b_ref[level, tile, :],
                tile_at,
                tiles,
                lambda start: b_ref[level, pl.ds(start, 8), :],
                sides_s[level, tile, :],
                lambda: north_s[pl.ds(2 * level + 1, 8), :],
                lambda: north_s[pl.ds(2 * level + 2, 8), :],
                lambda: south_s[pl.ds(2 * level + 9, 8), :],
                lambda: south_s[pl.ds(2 * level + 8, 8), :],
            )
            weight = jnp.where(level.astype(F32) < counts_s[pl.ds(8 + 8 * tile_at, 8), :], thick, 0.0)
            forcing[tile_at] = forcing[tile_at] + weight * value
            depth_sum[tile_at] = depth_sum[tile_at] + weight
        return tuple(forcing), tuple(depth_sum)

    zeros = tuple(jnp.zeros((8, width), F32) for _ in range(tiles))
    forcing, depth_sum = lax.fori_loop(0, levels, level_body, (zeros, zeros), unroll=4)
    for at in range(tiles):
        tile = pl.ds(8 * at, 8)
        ocean = jnp.where(counts_s[pl.ds(8 + 8 * at, 8), :] > 0.0, 1.0, 0.0)
        fields_ref[0, tile, :] = ocean * (0.5 * forcing[at] + surface_ref[tile, :])
        fields_ref[1, tile, :] = pressure_ref[tile, :]
        fields_ref[2, tile, :] = 5.0 + 2.0 / (1.0 + depth_sum[at])


def shift_matrix():
    shape = (256, 256)
    column = lanes(shape)
    offset = rows(shape) % 128 - column % 128
    near = jnp.where(offset == 1, 1.0, 0.0)
    far = jnp.where(offset == -1, 1.0, 0.0)
    both = jnp.where(offset == 2, 1.0, 0.0) - jnp.where(offset == -2, 1.0, 0.0)
    return jnp.where(column < 128, near + far, 8.0 * (near - far) - both).astype(jnp.bfloat16)


def side_kernel(masks_ref, u_ref, depth_ref, x_first_ref, x_second_ref, sides_ref):
    kinds = x_first_ref.shape[0]
    levels, height, width = u_ref.shape
    half = levels // 2
    even_x = is_even("gx")
    spot = lanes((height, width)) % 4
    column = lanes((height, width))
    for group in range(2):
        near, far = jnp.zeros((height, width), F32), jnp.zeros((height, width), F32)
        for at in range(half):
            level = group * half + at
            mixing = depth_ref[level] * masks_ref[8]
            u8, u1 = u_ref[level] * (8.0 / 12.0), u_ref[level] * (1.0 / 12.0)
            first = jnp.where(
                column == width - 1,
                jnp.where(level < masks_ref[0], mixing - u8, 0.0),
                jnp.where(level < masks_ref[1], mixing + u8, 0.0),
            )
            first = jnp.where((column == 0) | (column == width - 1), first, 0.0)
            second = jnp.where(
                column < 2, jnp.where(level < masks_ref[3], -u1, 0.0), jnp.where(level < masks_ref[2], u1, 0.0)
            )
            here = column // 4 == at
            near = jnp.where(here, roll(first, 4 * at - 126, 1), near)
            far = jnp.where(here, roll(second, 4 * at - 126, 1), far)
        for kind in range(kinds):
            x_first, x_second = x_first_ref[kind], x_second_ref[kind]
            values = unpack_groups(jnp.where(even_x, x_second, x_first), jnp.where(even_x, x_first, x_second))[group]
            by_two = jnp.where(spot < 2, roll(values, -2, 1), roll(values, 2, 1))
            by_one = jnp.where(spot < 2, roll(values, -1, 1), roll(values, 1, 1))
            sides_ref[kind, group] = near * by_one + far * by_two


def advance_kernel(
    tracers_ref,
    u_ref,
    v_ref,
    depth_ref,
    masks_ref,
    counts_ref,
    sides_ref,
    y_first_ref,
    y_second_ref,
    out_ref,
    held,
    masked_s,
    parts_s,
    moved_s,
    matrix_s,
    weights_s,
    in_semaphore,
    out_semaphore,
):
    kinds, levels, height, width = tracers_ref.shape
    groups = in_semaphore.shape[0]
    chunk = levels // groups
    tiles = height // 8
    half = levels // 2

    def load(group):
        where = (slice(None), pl.ds(group * chunk, chunk))
        return pltpu.make_async_copy(tracers_ref.at[where], held.at[where], in_semaphore.at[group])

    def store(group):
        where = (slice(None), pl.ds(group * chunk, chunk))
        return pltpu.make_async_copy(held.at[where], out_ref.at[where], out_semaphore.at[group])

    for group in range(groups):
        load(group).start()
    matrix_s[...] = shift_matrix()
    even_y = is_even("gy")
    column = lanes((8, width))
    outer = (column < 2) | (column >= width - 2)

    def prepare(level, at):
        number = level.astype(F32)
        for tile_at in range(tiles):
            tile = pl.ds(8 * tile_at, 8)
            mixing = depth_ref[level] * masks_ref[8, tile, :]
            u, v = u_ref[level, tile, :], v_ref[level, tile, :]
            active = number < counts_ref[pl.ds(8 + 8 * tile_at, 8), :]
            weights_s[at, 0, tile, :] = weights_of(level, mixing, tile, masks_ref, u, v)[1]
            weights_s[at, 1, tile, :] = jnp.where(active, mixing, 0.0)
            weights_s[at, 2, tile, :] = jnp.where(active, u * (-1.0 / 12.0), 0.0)
            weights_s[at, 3, tile, :] = jnp.where(active, v * (-1.0 / 12.0), 0.0)
        active = number < counts_ref[8 : 8 + height, :]
        south_active = number < counts_ref[6:8, :]
        north_active = number < counts_ref[8 + height : 10 + height, :]
        for kind in range(kinds):
            seen = jnp.where(active, held[kind, level], 0.0)
            masked_s[at, kind, 8 : 8 + height, :] = seen
            high = seen.astype(jnp.bfloat16)
            row = (at * kinds + kind) * height
            parts_s[row : row + height, 0:width] = high
            parts_s[row : row + height, width : 2 * width] = (seen - high.astype(F32)).astype(jnp.bfloat16)
            first, second = (ref[kind, pl.ds(2 * level, 2), :] for ref in (y_first_ref, y_second_ref))
            north = jnp.where(even_y, first, second)
            south = jnp.where(even_y, second, first)
            masked_s[at, kind, 8 + height : 10 + height, :] = jnp.where(north_active, north, 0.0)
            masked_s[at, kind, 6:8, :] = jnp.where(south_active, south, 0.0)

    def finish(level, at):
        group = level // half
        shift = 126 - 4 * (level - half * group)
        for tile_at in range(tiles):
            base = 8 * tile_at
            tile = pl.ds(base, 8)
            own_weight, mixing, eastward, northward = (weights_s[at, i, tile, :] for i in range(4))
            for kind in range(kinds):
                row = (at * kinds + kind) * height + base
                n1, s1, n2, s2 = (masked_s[at, kind, pl.ds(8 + base + by, 8), :] for by in (1, -1, 2, -2))
                side = jnp.where(outer, pltpu.roll(sides_ref[kind, group, tile, :], shift, 1), 0.0)
                held[kind, level, tile, :] = (
                    own_weight * held[kind, level, tile, :]
                    + mixing * (moved_s[row : row + 8, 0:width] + (n1 + s1))
                    + eastward * moved_s[row : row + 8, width : 2 * width]
                    + northward * (8.0 * (n1 - s1) - (n2 - s2))
                    + side
                )

    def one_group(group, carry):
        load(group).wait()
        for at in range(chunk):
            prepare(group * chunk + at, at)
        moved_s[...] = jnp.dot(parts_s[...], matrix_s[...], preferred_element_type=F32)
        for at in range(chunk):
            finish(group * chunk + at, at)
        store(group).start()
        return carry

    lax.fori_loop(0, groups, one_group, 0)
    for group in range(groups):
        store(group).wait()


def outer_rows_kernel(fields_ref, x_first_ref, x_second_ref, side_ref, y_first_ref, y_second_ref):
    count, height, width = fields_ref.shape
    even_x, even_y = is_even("gx"), is_even("gy")
    eastern = (lanes((height, width)) < width // 2) == even_x
    for at in range(count):
        side = jnp.where(eastern, x_first_ref[at], x_second_ref[at])
        side_ref[at] = side
        for place, values in ((at, fields_ref[at]), (count + at, side)):
            low, high = values[0:8, :], values[height - 8 : height, :]
            y_first_ref[place] = jnp.where(even_y, high, low)
            y_second_ref[place] = jnp.where(even_y, low, high)


def extended(fields_ref, side_ref, y_first_ref, y_second_ref, at):
    count = fields_ref.shape[0]
    even_y = is_even("gy")

    def column(inner, place):
        first, second = y_first_ref[place], y_second_ref[place]
        return jnp.concatenate([inner, jnp.where(even_y, first, second), jnp.where(even_y, second, first)], axis=0)

    return jnp.concatenate([column(fields_ref[at], at), column(side_ref[at], count + at)], axis=1)


def krylov_kernel(fields_ref, side_ref, y_first_ref, y_second_ref, basis_ref, sums_ref):
    height, width = fields_ref.shape[1], fields_ref.shape[2]
    forcing, pressure, center = (
        extended(fields_ref, side_ref, y_first_ref, y_second_ref, at) for at in range(3)
    )
    shape = forcing.shape
    column, row = lanes(shape), rows(shape)
    gx, gy = lax.axis_index("gx"), lax.axis_index("gy")
    end_x, end_y = lax.axis_size("gx") - 1, lax.axis_size("gy") - 1
    least_column = jnp.where(gx < end_x, 0, width)
    most_column = jnp.where(gx > 0, 2 * width, width + width // 2)
    least_row = jnp.where(gy < end_y, 0, height)
    most_row = jnp.where(gy > 0, height + 16, height + 8)
    inside_x = (column < width) | ((column >= least_column) & (column < width + width // 2) & (gx < end_x)) | (
        (column >= width + width // 2) & (column < most_column)
    )
    inside_y = (row < height) | ((row >= least_row) & (row < height + 8) & (gy < end_y)) | (
        (row >= height + 8) & (row < most_row)
    )
    ocean = jnp.where((center < 6.75) & inside_x & inside_y, 1.0, 0.0)
    diagonal = jnp.where(ocean > 0.0, center, 1.0)

    def operate(values):
        seen = ocean * values
        beside = roll(seen, 1, 1) + roll(seen, -1, 1)
        mixed = seen + 0.25 * beside
        return diagonal * values - ocean * (beside + (roll(mixed, 1, 0) + roll(mixed, -1, 0)))

    def scaled(values):
        return 0.2 * operate(values) - values

    base = [forcing - operate(pressure)]
    base.append(scaled(base[0]))
    base.append(2.0 * scaled(base[1]) - base[0])
    base.append(2.0 * scaled(base[2]) - base[1])
    last = scaled(base[3])
    for at in range(4):
        basis_ref[at] = base[at]
    basis_ref[4] = pressure
    basis_ref[5] = ocean
    inner = [values[0:height, 0:width] for values in base]
    sums = []
    for at in range(4):
        for other in range(at + 1):
            sums.append(inner[at] * inner[other])
    sums.append(inner[3] * last[0:height, 0:width])
    line = jnp.zeros((8, width), F32)
    for at, values in enumerate(sums):
        part = values[0:8]
        for start in range(8, height, 8):
            part = part + values[start : start + 8]
        total = jnp.sum(jnp.sum(part, axis=0, keepdims=True), axis=1, keepdims=True)
        line = jnp.where(lanes(line.shape) == at, total, line)
    for start in range(0, sums_ref.shape[0], 8):
        sums_ref[start : start + 8, :] = line


def finish_kernel(basis_ref, sums_ref, pressure_ref, gradient_ref):
    height, width = pressure_ref.shape
    part = sums_ref[0:8, :]
    for start in range(8, sums_ref.shape[0], 8):
        part = part + sums_ref[start : start + 8, :]
    line = jnp.sum(part, axis=0, keepdims=True)

    def entry(at):
        return jnp.sum(jnp.where(lanes(line.shape) == at, line, 0.0), axis=1, keepdims=True)

    gram = [[None] * 4 for _ in range(4)]
    at = 0
    for i in range(4):
        for j in range(i + 1):
            gram[i][j] = gram[j][i] = entry(at)
            at += 1
    tail = entry(at)

    def scaled(coef):
        out = [None] * 5
        for j, value in enumerate(coef):
            if value is None:
                continue
            moves = [(1, value)] if j == 0 else [(j + 1, 0.5 * value), (j - 1, 0.5 * value)]
            for place, amount in moves:
                out[place] = amount if out[place] is None else out[place] + amount
        return out

    def dot(left, right):
        total = None
        for i in range(4):
            for j in range(4):
                if left[i] is None or right[j] is None:
                    continue
                term = left[i] * right[j] * gram[i][j]
                total = term if total is None else total + term
        return total

    def plus(left, factor, right):
        out = []
        for a, b in zip(left, right):
            if b is None:
                out.append(a)
            elif a is None:
                out.append(factor * b)
            else:
                out.append(a + factor * b)
        return out

    one = jnp.ones_like(tail)
    residual = [one, None, None, None]
    direction = [one, None, None, None]
    solution_coef = [None] * 4
    norm = dot(residual, residual)
    for step in range(ITERS):
        moved = scaled(direction)
        if step < ITERS - 1:
            energy = dot(direction, moved[:4])
        else:
            low = direction[:3] + [None]
            moved_low = scaled(low)[:4]
            energy = (
                dot(low, moved_low)
                + 2.0 * direction[3] * dot([None, None, None, one], moved_low)
                + direction[3] * direction[3] * tail
            )
        energy = 5.0 * (energy + dot(direction, direction))
        factor = norm / energy
        solution_coef = plus(solution_coef, factor, direction)
        if step < ITERS - 1:
            image = plus([None if m is None else 5.0 * m for m in moved[:4]], 5.0, direction)
            residual = plus(residual, -factor, image)
            new = dot(residual, residual)
            direction = plus(residual, new / norm, direction)
            norm = new

    pressure = basis_ref[4]
    for j in range(4):
        pressure = pressure + solution_coef[j] * basis_ref[j]
    ocean = basis_ref[5]
    seen = ocean * pressure
    half = 0.5 * ocean
    east = half * (roll(seen, -1, 1) - roll(seen, 1, 1))
    north = half * (roll(seen, -1, 0) - roll(seen, 1, 0))
    pressure_ref[...] = pressure[0:height, 0:width]
    gradient_ref[0] = east[0:height, 0:width]
    gradient_ref[1] = north[0:height, 0:width]


def exchange(first, second, axis):
    wide, tall = lax.axis_size("gx"), lax.axis_size("gy")
    pairs, others = [], []
    for x in range(wide):
        for y in range(tall):
            at = x * tall + y
            if axis == "gx":
                pairs.append((at, (x ^ 1) * tall + y))
                others.append((at, ((x + 1 if x % 2 else x - 1) % wide) * tall + y))
            else:
                pairs.append((at, x * tall + (y ^ 1)))
                beyond = y + 1 if y % 2 else y - 1
                inside = 0 <= beyond < tall
                others.append((at, x * tall + beyond if inside else (x ^ 1) * tall + y))
    return lax.ppermute(first, AXES, pairs), lax.ppermute(second, AXES, others)


def full(shape):
    return pl.BlockSpec(shape, lambda *_: (0,) * len(shape))


def vmem():
    return pl.BlockSpec(memory_space=pltpu.VMEM)


def hbm():
    return pl.BlockSpec(memory_space=pltpu.HBM)


def smem():
    return pl.BlockSpec(memory_space=pltpu.SMEM)


def params(limit=32, **more):
    return pltpu.CompilerParams(vmem_limit_bytes=limit * MIB, **more)


def struct(*shape):
    return jax.ShapeDtypeStruct(shape, F32)


def per_device(
    tracers,
    level_counts,
    u_vel,
    v_vel,
    diff_depth,
    diff_lat,
    thickness,
    surface_forcing,
    initial_pressure,
):
    kinds, levels, height, width = tracers.shape
    packed = 2 * levels
    with jax.named_scope("pack_buoyancy"):
        buoyancy, x_first, x_second, y_first, y_second = pl.pallas_call(
            pack_buoyancy_kernel,
            in_specs=[hbm(), hbm()],
            out_shape=[
                struct(levels, height, width),
                struct(2, height, width),
                struct(2, height, width),
                struct(packed + 16, width),
                struct(packed + 16, width),
            ],
            scratch_shapes=[
                pltpu.VMEM((2, levels, height, width), F32),
                pltpu.VMEM((height, width), jnp.int32),
                pltpu.SemaphoreType.DMA((8,)),
                pltpu.SemaphoreType.DMA,
            ],
            compiler_params=params(52),
        )(tracers, level_counts)
    with jax.named_scope("buoyancy_halo"):
        x_halo = exchange(x_first, x_second, "gx")
        y_halo = exchange(y_first, y_second, "gy")
    with jax.named_scope("pack_tracers"):
        early = kinds // 2
        later, _ = lax.optimization_barrier((tracers, x_first))
        packs = pack_tracers(later, 0, early)
        buoyancy, *packs = lax.optimization_barrier((buoyancy, *packs))
    with jax.named_scope("forcing"):
        fields, masks, counts = pl.pallas_call(
            forcing_kernel,
            in_specs=[vmem()] * 4 + [smem()] * 3 + [vmem()] * 6,
            out_shape=[struct(3, height, width), struct(9, height, width), struct(height + 16, width)],
            scratch_shapes=[
                pltpu.VMEM((levels, height, width), F32),
                pltpu.VMEM((packed + 16, width), F32),
                pltpu.VMEM((packed + 16, width), F32),
            ],
            compiler_params=params(8),
        )(
            buoyancy,
            level_counts,
            u_vel,
            v_vel,
            diff_depth,
            diff_lat,
            thickness,
            surface_forcing,
            initial_pressure,
            *x_halo,
            *y_halo,
        )
    with jax.named_scope("fields_halo"):
        f_x_halo = exchange(fields, fields, "gx")
        later, _ = lax.optimization_barrier((tracers, fields))
        packs = pack_tracers(later, early, kinds - early, packs)
        own_fields, *packs = lax.optimization_barrier((fields, *packs))
        side, f_y_first, f_y_second = pl.pallas_call(
            outer_rows_kernel,
            out_shape=[struct(3, height, width), struct(6, 8, width), struct(6, 8, width)],
            compiler_params=params(4),
        )(own_fields, *f_x_halo)
        f_y_halo = exchange(f_y_first, f_y_second, "gy")
    with jax.named_scope("tracer_halo"):
        t_x_first, t_x_second, t_y_first, t_y_second = packs
        t_x_halo = exchange(t_x_first, t_x_second, "gx")
        *f_y_halo, t_y_first, t_y_second = lax.optimization_barrier((*f_y_halo, t_y_first, t_y_second))
        t_y_halo = exchange(t_y_first, t_y_second, "gy")
    with jax.named_scope("krylov"):
        basis, sums = pl.pallas_call(
            krylov_kernel,
            out_shape=[struct(6, height + 16, 2 * width), struct(128, width)],
            compiler_params=params(8),
        )(fields, side, *f_y_halo)
        all_sums = lax.all_to_all(sums, AXES, 0, 0, tiled=True)
        masks, _ = lax.optimization_barrier((masks, sums))
    with jax.named_scope("side_terms"):
        sides = pl.pallas_call(
            side_kernel,
            in_specs=[vmem(), vmem(), smem(), vmem(), vmem()],
            out_shape=struct(kinds, 2, height, width),
            compiler_params=params(8),
            cost_estimate=pl.CostEstimate(flops=4_000_000, bytes_accessed=3_000_000, transcendentals=0),
        )(masks, u_vel, diff_depth, *t_x_halo)
    chunk = 4
    with jax.named_scope("advance"):
        new_tracers = pl.pallas_call(
            advance_kernel,
            in_specs=[hbm(), vmem(), vmem(), smem()] + [vmem()] * 5,
            out_specs=hbm(),
            out_shape=struct(kinds, levels, height, width),
            scratch_shapes=[
                pltpu.VMEM((kinds, levels, height, width), F32),
                pltpu.VMEM((chunk, kinds, height + 16, width), F32),
                pltpu.VMEM((chunk * kinds * height, 2 * width), jnp.bfloat16),
                pltpu.VMEM((chunk * kinds * height, 2 * width), F32),
                pltpu.VMEM((2 * width, 2 * width), jnp.bfloat16),
                pltpu.VMEM((chunk, 4, height, width), F32),
                pltpu.SemaphoreType.DMA((levels // chunk,)),
                pltpu.SemaphoreType.DMA((levels // chunk,)),
            ],
            compiler_params=params(52),
            cost_estimate=pl.CostEstimate(flops=60_000_000, bytes_accessed=22_000_000, transcendentals=0),
        )(tracers, u_vel, v_vel, diff_depth, masks, counts, sides, *t_y_halo)
    with jax.named_scope("solve"):
        new_tracers, all_sums = lax.optimization_barrier((new_tracers, all_sums))
        pressure, gradient = pl.pallas_call(
            finish_kernel,
            out_shape=[struct(height, width), struct(2, height, width)],
            compiler_params=params(8),
        )(basis, all_sums)
    return new_tracers, pressure, gradient


def solution(mesh):
    return jax.shard_map(
        per_device,
        mesh=mesh,
        in_specs=(
            P(None, None, "gy", "gx"),
            P("gy", "gx"),
            P(None, "gy", "gx"),
            P(None, "gy", "gx"),
            P(),
            P("gy"),
            P(),
            P("gy", "gx"),
            P("gy", "gx"),
        ),
        out_specs=(P(None, None, "gy", "gx"), P("gy", "gx"), P(None, "gy", "gx")),
        check_vma=False,
    )
```

```python
import functools

import jax
import jax.numpy as jnp
from jax import lax
from jax.experimental import pallas as pl
from jax.experimental.pallas import tpu as pltpu
from jax.sharding import PartitionSpec as P

ITERS = 4
F32 = jnp.float32
AXES = ("gx", "gy")
MIB = 1024 * 1024


def roll(values, shift, axis):
    size = values.shape[axis]
    if isinstance(shift, int):
        shift = shift % size
        if shift == 0:
            return values
    return pltpu.roll(values, shift, axis)


def lanes(shape):
    return lax.broadcasted_iota(jnp.int32, shape, len(shape) - 1)


def rows(shape):
    return lax.broadcasted_iota(jnp.int32, shape, len(shape) - 2)


def pack_columns(load, levels):
    half = levels // 2
    groups = []
    for group in range(2):
        packed = None
        for at in range(half):
            values = load(group * half + at)
            moved = roll(values, 4 * at - 126, 1)
            if packed is None:
                packed = moved
            else:
                packed = jnp.where(lanes(moved.shape) // 4 == at, moved, packed)
        groups.append(packed)
    low = lanes(groups[0].shape) % 4 < 2
    last = jnp.where(low, groups[0], roll(groups[1], 2, 1))
    first = jnp.where(low, roll(groups[0], -2, 1), groups[1])
    return last, first


def unpack_groups(from_west, from_east):
    low = lanes(from_west.shape) % 4 < 2
    return (
        jnp.where(low, from_west, roll(from_east, 2, 1)),
        jnp.where(low, roll(from_west, -2, 1), from_east),
    )


def is_even(axis):
    return lax.axis_index(axis) % 2 == 0


def copy_in(source, place, semaphore, parts):
    copies = []
    size = source.shape[0] // parts
    for part in range(parts):
        where = pl.ds(part * size, size)
        copies.append(pltpu.make_async_copy(source.at[where], place.at[where], semaphore.at[part]))
        copies[-1].start()
    return copies


def pack_buoyancy_kernel(
    tracers_ref,
    counts_ref,
    b_ref,
    x_first_ref,
    x_second_ref,
    y_first_ref,
    y_second_ref,
    held,
    counts_s,
    semaphore,
    counts_semaphore,
):
    levels, height = b_ref.shape[0], b_ref.shape[1]
    parts = semaphore.shape[0] // 2
    warm = copy_in(tracers_ref.at[0], held.at[0], semaphore.at[pl.ds(0, parts)], parts)
    salt = copy_in(tracers_ref.at[1], held.at[1], semaphore.at[pl.ds(parts, parts)], parts)
    counts_copy = pltpu.make_async_copy(counts_ref, counts_s, counts_semaphore)
    counts_copy.start()
    even_x, even_y = is_even("gx"), is_even("gy")

    def load(level):
        if level % (levels // parts) == 0:
            warm[level // (levels // parts)].wait()
            salt[level // (levels // parts)].wait()
        values = 0.2 * held[0, level] - 0.8 * held[1, level]
        b_ref[level] = values
        high, low = values[height - 2 : height, :], values[0:2, :]
        y_first_ref[8 + 2 * level : 10 + 2 * level, :] = jnp.where(even_y, high, low)
        y_second_ref[8 + 2 * level : 10 + 2 * level, :] = jnp.where(even_y, low, high)
        return values

    last, first = pack_columns(load, levels)
    x_first_ref[0] = jnp.where(even_x, last, first)
    x_second_ref[0] = jnp.where(even_x, first, last)
    counts_copy.wait()
    counts = counts_s[...].astype(F32)
    x_first_ref[1] = counts
    x_second_ref[1] = counts
    low, high = counts[0:8, :], counts[height - 8 : height, :]
    for start in (0, 8 + 2 * levels):
        y_first_ref[start : start + 8, :] = jnp.where(even_y, high, low)
        y_second_ref[start : start + 8, :] = jnp.where(even_y, low, high)


def pack_tracers_kernel(first_kind, tracers_ref, *refs):
    x_first_ref, x_second_ref, y_first_ref, y_second_ref, held, semaphore = refs[-6:]
    kinds, levels, height, width = held.shape
    even_x, even_y = is_even("gx"), is_even("gy")

    flat = held.reshape(kinds * levels * height, width)

    def copy(kind):
        return pltpu.make_async_copy(tracers_ref.at[first_kind + kind], held.at[kind], semaphore.at[kind])

    for kind in range(kinds):
        copy(kind).start()
    for before_ref, ref in zip(refs[:-6], refs[-6:-2]):
        ref[0:first_kind] = before_ref[...]

    def one_kind(kind, carry):
        copy(kind).wait()
        place = first_kind + kind

        for side_row in range(2):
            for start in range(0, levels, 8):
                base = (kind * levels + start) * height + side_row
                high = flat[pl.ds(base + height - 2, 8, stride=height), :]
                low = flat[pl.ds(base, 8, stride=height), :]
                tile = pl.ds(side_row * levels + start, 8)
                y_first_ref[place, tile, :] = jnp.where(even_y, high, low)
                y_second_ref[place, tile, :] = jnp.where(even_y, low, high)
        last, first = pack_columns(lambda level: held[kind, level], levels)
        x_first_ref[place] = jnp.where(even_x, last, first)
        x_second_ref[place] = jnp.where(even_x, first, last)
        return carry

    lax.fori_loop(0, kinds, one_kind, 0)


def pack_tracers(tracers, first_kind, count, before=()):
    kinds, levels, height, width = tracers.shape
    upto = first_kind + count
    return pl.pallas_call(
        functools.partial(pack_tracers_kernel, first_kind),
        in_specs=[hbm()] + [vmem()] * len(before),
        out_shape=[struct(upto, height, width)] * 2 + [struct(upto, 2 * levels, width)] * 2,
        scratch_shapes=[pltpu.VMEM((count, levels, height, width), F32), pltpu.SemaphoreType.DMA((count,))],
        compiler_params=params(52),
        cost_estimate=pl.CostEstimate(flops=10_000_000, bytes_accessed=6_000_000, transcendentals=0),
    )(tracers, *before)


def weights_of(level, mixing, tile, masks_ref, u, v):
    u8, u1 = u * (8.0 / 12.0), u * (1.0 / 12.0)
    v8, v1 = v * (8.0 / 12.0), v * (1.0 / 12.0)
    plain = (mixing - u8, mixing + u8, u1, -u1, mixing - v8, mixing + v8, v1, -v1)
    height = level.astype(F32)
    out = [jnp.where(height < masks_ref[at, tile, :], plain[at], 0.0) for at in range(8)]
    total = out[0]
    for weight in out[1:]:
        total = total + weight
    return out, 1.0 - total


def stencil(weights, own, tile_at, tiles, load_at, side, north_1, north_2, south_1, south_2):
    column = lanes(own.shape)
    row = rows(own.shape)
    base = 8 * tile_at
    width = own.shape[1]
    if tile_at + 1 < tiles:
        n1, n2 = load_at(base + 1), load_at(base + 2)
    else:
        n1 = jnp.where(row == 7, north_1(), roll(own, -1, 0))
        n2 = jnp.where(row >= 6, north_2(), roll(own, -2, 0))
    if tile_at > 0:
        s1, s2 = load_at(base - 1), load_at(base - 2)
    else:
        s1 = jnp.where(row == 0, south_1(), roll(own, 1, 0))
        s2 = jnp.where(row < 2, south_2(), roll(own, 2, 0))
    near, middle = weights
    total = middle * own
    for weight, value in zip(
        near,
        (
            roll(jnp.where(column < 1, side, own), -1, 1),
            roll(jnp.where(column >= width - 1, side, own), 1, 1),
            roll(jnp.where(column < 2, side, own), -2, 1),
            roll(jnp.where(column >= width - 2, side, own), 2, 1),
            n1,
            s1,
            n2,
            s2,
        ),
    ):
        total = total + weight * value
    return total


def table_parts(tables_ref, levels):
    planes, height, width = tables_ref.shape
    flat = tables_ref.reshape(planes * height, width)
    start = 9 * height
    return flat.at[pl.ds(start, height + 16)], flat.at[pl.ds(start + height + 16, levels)]


def forcing_kernel(
    b_ref,
    counts_ref,
    u_ref,
    v_ref,
    depth_ref,
    lat_ref,
    thick_ref,
    surface_ref,
    pressure_ref,
    x_first_ref,
    x_second_ref,
    y_first_ref,
    y_second_ref,
    fields_ref,
    masks_ref,
    sides_s,
    north_s,
    south_s,
):
    levels, height, width = b_ref.shape
    tiles = height // 8
    half = levels // 2
    counts_s, depths_ref = table_parts(masks_ref, levels)
    gx, gy = lax.axis_index("gx"), lax.axis_index("gy")
    even_x, even_y = is_even("gx"), is_even("gy")
    end_x, end_y = lax.axis_size("gx") - 1, lax.axis_size("gy") - 1
    counts = counts_ref[...].astype(F32)
    column = lanes(counts.shape)
    east = jnp.where(even_x, x_first_ref[1], x_second_ref[1]) * jnp.where(gx < end_x, 1.0, 0.0)
    west = jnp.where(even_x, x_second_ref[1], x_first_ref[1]) * jnp.where(gx > 0, 1.0, 0.0)
    north_s[...] = jnp.where(even_y, y_first_ref[...], y_second_ref[...])
    south_s[...] = jnp.where(even_y, y_second_ref[...], y_first_ref[...])
    masks_ref[0] = jnp.minimum(counts, roll(jnp.where(column < 1, east, counts), -1, 1))
    masks_ref[1] = jnp.minimum(counts, roll(jnp.where(column >= width - 1, west, counts), 1, 1))
    masks_ref[2] = jnp.minimum(counts, roll(jnp.where(column < 2, east, counts), -2, 1))
    masks_ref[3] = jnp.minimum(counts, roll(jnp.where(column >= width - 2, west, counts), 2, 1))
    counts_s[0:8, :] = south_s[0:8, :] * jnp.where(gy > 0, 1.0, 0.0)
    counts_s[8 : 8 + height, :] = counts
    counts_s[8 + height : 16 + height, :] = north_s[0:8, :] * jnp.where(gy < end_y, 1.0, 0.0)
    masks_ref[4] = jnp.minimum(counts, counts_s[9 : 9 + height, :])
    masks_ref[5] = jnp.minimum(counts, counts_s[7 : 7 + height, :])
    masks_ref[6] = jnp.minimum(counts, counts_s[10 : 10 + height, :])
    masks_ref[7] = jnp.minimum(counts, counts_s[6 : 6 + height, :])
    for level in range(levels):
        depths_ref[level : level + 1, :] = jnp.full((1, width), depth_ref[level], F32)
    row = rows(counts.shape)
    lat = jnp.zeros(counts.shape, F32)
    for at in range(height):
        lat = jnp.where(row == at, lat_ref[at], lat)
    masks_ref[8] = lat
    groups = unpack_groups(
        jnp.where(even_x, x_second_ref[0], x_first_ref[0]), jnp.where(even_x, x_first_ref[0], x_second_ref[0])
    )
    for level in range(levels):
        sides_s[level] = roll(groups[level // half], 126 - 4 * (level % half), 1)

    def level_body(level, carry):
        thick = thick_ref[level]
        forcing, depth_sum = list(carry[0]), list(carry[1])
        for tile_at in range(tiles):
            tile = pl.ds(8 * tile_at, 8)
            mixing = depth_ref[level] * masks_ref[8, tile, :]
            weights = weights_of(level, mixing, tile, masks_ref, u_ref[level, tile, :], v_ref[level, tile, :])
            value = stencil(
                weights,
                b_ref[level, tile, :],
                tile_at,
                tiles,
                lambda start: b_ref[level, pl.ds(start, 8), :],
                sides_s[level, tile, :],
                lambda: north_s[pl.ds(2 * level + 1, 8), :],
                lambda: north_s[pl.ds(2 * level + 2, 8), :],
                lambda: south_s[pl.ds(2 * level + 9, 8), :],
                lambda: south_s[pl.ds(2 * level + 8, 8), :],
            )
            weight = jnp.where(level.astype(F32) < counts_s[pl.ds(8 + 8 * tile_at, 8), :], thick, 0.0)
            forcing[tile_at] = forcing[tile_at] + weight * value
            depth_sum[tile_at] = depth_sum[tile_at] + weight
        return tuple(forcing), tuple(depth_sum)

    zeros = tuple(jnp.zeros((8, width), F32) for _ in range(tiles))
    forcing, depth_sum = lax.fori_loop(0, levels, level_body, (zeros, zeros), unroll=4)
    for at in range(tiles):
        tile = pl.ds(8 * at, 8)
        ocean = jnp.where(counts_s[pl.ds(8 + 8 * at, 8), :] > 0.0, 1.0, 0.0)
        fields_ref[0, tile, :] = ocean * (0.5 * forcing[at] + surface_ref[tile, :])
        fields_ref[1, tile, :] = pressure_ref[tile, :]
        fields_ref[2, tile, :] = 5.0 + 2.0 / (1.0 + depth_sum[at])


def shift_matrix():
    shape = (256, 256)
    column = lanes(shape)
    offset = rows(shape) % 128 - column % 128
    near = jnp.where(offset == 1, 1.0, 0.0)
    far = jnp.where(offset == -1, 1.0, 0.0)
    both = jnp.where(offset == 2, 1.0, 0.0) - jnp.where(offset == -2, 1.0, 0.0)
    return jnp.where(column < 128, near + far, 8.0 * (near - far) - both).astype(jnp.bfloat16)


def side_weights_kernel(masks_ref, u_ref, weights_ref):
    levels, height, width = u_ref.shape
    half = levels // 2
    depths_ref = table_parts(masks_ref, levels)[1]
    column = lanes((height, width))
    for group in range(2):
        near, far = jnp.zeros((height, width), F32), jnp.zeros((height, width), F32)
        for at in range(half):
            level = group * half + at
            mixing = depths_ref[level : level + 1, :] * masks_ref[8]
            u8, u1 = u_ref[level] * (8.0 / 12.0), u_ref[level] * (1.0 / 12.0)
            first = jnp.where(
                column == width - 1,
                jnp.where(level < masks_ref[0], mixing - u8, 0.0),
                jnp.where(level < masks_ref[1], mixing + u8, 0.0),
            )
            first = jnp.where((column == 0) | (column == width - 1), first, 0.0)
            second = jnp.where(
                column < 2, jnp.where(level < masks_ref[3], -u1, 0.0), jnp.where(level < masks_ref[2], u1, 0.0)
            )
            here = column // 4 == at
            near = jnp.where(here, roll(first, 4 * at - 126, 1), near)
            far = jnp.where(here, roll(second, 4 * at - 126, 1), far)
        weights_ref[group, 0] = near
        weights_ref[group, 1] = far


def side_kernel(weights_ref, x_first_ref, x_second_ref, sides_ref):
    kinds, height, width = x_first_ref.shape
    even_x = is_even("gx")
    spot = lanes((height, width)) % 4
    for kind in range(kinds):
        x_first, x_second = x_first_ref[kind], x_second_ref[kind]
        groups = unpack_groups(jnp.where(even_x, x_second, x_first), jnp.where(even_x, x_first, x_second))
        for group, values in enumerate(groups):
            by_two = jnp.where(spot < 2, roll(values, -2, 1), roll(values, 2, 1))
            by_one = jnp.where(spot < 2, roll(values, -1, 1), roll(values, 1, 1))
            sides_ref[kind, group] = weights_ref[group, 0] * by_one + weights_ref[group, 1] * by_two


def advance_kernel(
    tracers_ref,
    u_ref,
    v_ref,
    masks_ref,
    sides_ref,
    y_first_ref,
    y_second_ref,
    out_ref,
    held,
    masked_s,
    parts_s,
    moved_s,
    matrix_s,
    weights_s,
    north_s,
    south_s,
    in_semaphore,
    out_semaphore,
):
    kinds, levels, height, width = tracers_ref.shape
    groups = in_semaphore.shape[0]
    chunk = levels // groups
    tiles = height // 8
    half = levels // 2
    counts_ref, depths_ref = table_parts(masks_ref, levels)

    def load(group):
        where = (slice(None), pl.ds(group * chunk, chunk))
        return pltpu.make_async_copy(tracers_ref.at[where], held.at[where], in_semaphore.at[group])

    def store(group):
        where = (slice(None), pl.ds(group * chunk, chunk))
        return pltpu.make_async_copy(held.at[where], out_ref.at[where], out_semaphore.at[group])

    for group in range(groups):
        load(group).start()
    matrix_s[...] = shift_matrix()
    even_y = is_even("gy")
    for side_row in range(2):
        south_counts = counts_ref[6 + side_row : 7 + side_row, :]
        north_counts = counts_ref[8 + height + side_row : 9 + height + side_row, :]
        for start in range(0, levels, 8):
            number = (rows((8, width)) + start).astype(F32)
            in_north, in_south = number < north_counts, number < south_counts
            tile = pl.ds(side_row * levels + start, 8)
            for kind in range(kinds):
                first, second = y_first_ref[kind, tile, :], y_second_ref[kind, tile, :]
                into = pl.ds(2 * (kind * levels + start) + side_row, 8, stride=2)
                north_s[into, :] = jnp.where(in_north, jnp.where(even_y, first, second), 0.0)
                south_s[into, :] = jnp.where(in_south, jnp.where(even_y, second, first), 0.0)
    column = lanes((8, width))
    outer = (column < 2) | (column >= width - 2)

    def prepare(level, at):
        number = level.astype(F32)
        for tile_at in range(tiles):
            tile = pl.ds(8 * tile_at, 8)
            mixing = depths_ref[pl.ds(level, 1), :] * masks_ref[8, tile, :]
            u, v = u_ref[level, tile, :], v_ref[level, tile, :]
            active = number < counts_ref[pl.ds(8 + 8 * tile_at, 8), :]
            weights_s[at, 0, tile, :] = weights_of(level, mixing, tile, masks_ref, u, v)[1]
            weights_s[at, 1, tile, :] = jnp.where(active, mixing, 0.0)
            weights_s[at, 2, tile, :] = jnp.where(active, u * (-1.0 / 12.0), 0.0)
            weights_s[at, 3, tile, :] = jnp.where(active, v * (-1.0 / 12.0), 0.0)
        active = number < counts_ref[8 : 8 + height, :]
        for kind in range(kinds):
            seen = jnp.where(active, held[kind, level], 0.0)
            masked_s[at, kind, 8 : 8 + height, :] = seen
            high = seen.astype(jnp.bfloat16)
            row = (at * kinds + kind) * height
            parts_s[row : row + height, 0:width] = high
            parts_s[row : row + height, width : 2 * width] = (seen - high.astype(F32)).astype(jnp.bfloat16)
            masked_s[at, kind, 8 + height : 10 + height, :] = north_s[pl.ds(2 * (kind * levels + level), 2), :]
            masked_s[at, kind, 6:8, :] = south_s[pl.ds(2 * (kind * levels + level), 2), :]

    def finish(level, at):
        group = level // half
        shift = 126 - 4 * (level - half * group)
        for tile_at in range(tiles):
            base = 8 * tile_at
            tile = pl.ds(base, 8)
            own_weight, mixing, eastward, northward = (weights_s[at, i, tile, :] for i in range(4))
            for kind in range(kinds):
                row = (at * kinds + kind) * height + base
                n1, s1, n2, s2 = (masked_s[at, kind, pl.ds(8 + base + by, 8), :] for by in (1, -1, 2, -2))
                side = jnp.where(outer, pltpu.roll(sides_ref[kind, group, tile, :], shift, 1), 0.0)
                held[kind, level, tile, :] = (
                    own_weight * held[kind, level, tile, :]
                    + mixing * (moved_s[row : row + 8, 0:width] + (n1 + s1))
                    + eastward * moved_s[row : row + 8, width : 2 * width]
                    + northward * (8.0 * (n1 - s1) - (n2 - s2))
                    + side
                )

    def one_group(group, carry):
        load(group).wait()
        for at in range(chunk):
            prepare(group * chunk + at, at)
        moved_s[...] = jnp.dot(parts_s[...], matrix_s[...], preferred_element_type=F32)
        for at in range(chunk):
            finish(group * chunk + at, at)
        store(group).start()
        return carry

    lax.fori_loop(0, groups, one_group, 0)
    for group in range(groups):
        store(group).wait()


def outer_rows_kernel(fields_ref, x_first_ref, x_second_ref, side_ref, y_first_ref, y_second_ref):
    count, height, width = fields_ref.shape
    even_x, even_y = is_even("gx"), is_even("gy")
    eastern = (lanes((height, width)) < width // 2) == even_x
    for at in range(count):
        side = jnp.where(eastern, x_first_ref[at], x_second_ref[at])
        side_ref[at] = side
        for place, values in ((at, fields_ref[at]), (count + at, side)):
            low, high = values[0:8, :], values[height - 8 : height, :]
            y_first_ref[place] = jnp.where(even_y, high, low)
            y_second_ref[place] = jnp.where(even_y, low, high)


def extended(fields_ref, side_ref, y_first_ref, y_second_ref, at):
    count = fields_ref.shape[0]
    even_y = is_even("gy")

    def column(inner, place):
        first, second = y_first_ref[place], y_second_ref[place]
        return jnp.concatenate([inner, jnp.where(even_y, first, second), jnp.where(even_y, second, first)], axis=0)

    return jnp.concatenate([column(fields_ref[at], at), column(side_ref[at], count + at)], axis=1)


def krylov_kernel(fields_ref, side_ref, y_first_ref, y_second_ref, basis_ref, sums_ref):
    height, width = fields_ref.shape[1], fields_ref.shape[2]
    forcing, pressure, center = (
        extended(fields_ref, side_ref, y_first_ref, y_second_ref, at) for at in range(3)
    )
    shape = forcing.shape
    column, row = lanes(shape), rows(shape)
    gx, gy = lax.axis_index("gx"), lax.axis_index("gy")
    end_x, end_y = lax.axis_size("gx") - 1, lax.axis_size("gy") - 1
    least_column = jnp.where(gx < end_x, 0, width)
    most_column = jnp.where(gx > 0, 2 * width, width + width // 2)
    least_row = jnp.where(gy < end_y, 0, height)
    most_row = jnp.where(gy > 0, height + 16, height + 8)
    inside_x = (column < width) | ((column >= least_column) & (column < width + width // 2) & (gx < end_x)) | (
        (column >= width + width // 2) & (column < most_column)
    )
    inside_y = (row < height) | ((row >= least_row) & (row < height + 8) & (gy < end_y)) | (
        (row >= height + 8) & (row < most_row)
    )
    ocean = jnp.where((center < 6.75) & inside_x & inside_y, 1.0, 0.0)
    diagonal = jnp.where(ocean > 0.0, center, 1.0)

    def operate(values):
        seen = ocean * values
        beside = roll(seen, 1, 1) + roll(seen, -1, 1)
        mixed = seen + 0.25 * beside
        return diagonal * values - ocean * (beside + (roll(mixed, 1, 0) + roll(mixed, -1, 0)))

    def scaled(values):
        return 0.2 * operate(values) - values

    base = [forcing - operate(pressure)]
    base.append(scaled(base[0]))
    base.append(2.0 * scaled(base[1]) - base[0])
    base.append(2.0 * scaled(base[2]) - base[1])
    last = scaled(base[3])
    for at in range(4):
        basis_ref[at] = base[at]
    basis_ref[4] = pressure
    basis_ref[5] = ocean
    inner = [values[0:height, 0:width] for values in base]
    sums = []
    for at in range(4):
        for other in range(at + 1):
            sums.append(inner[at] * inner[other])
    sums.append(inner[3] * last[0:height, 0:width])
    line = jnp.zeros((8, width), F32)
    for at, values in enumerate(sums):
        part = values[0:8]
        for start in range(8, height, 8):
            part = part + values[start : start + 8]
        total = jnp.sum(jnp.sum(part, axis=0, keepdims=True), axis=1, keepdims=True)
        line = jnp.where(lanes(line.shape) == at, total, line)
    for start in range(0, sums_ref.shape[0], 8):
        sums_ref[start : start + 8, :] = line


def finish_kernel(basis_ref, sums_ref, pressure_ref, gradient_ref):
    height, width = pressure_ref.shape
    part = sums_ref[0:8, :]
    for start in range(8, sums_ref.shape[0], 8):
        part = part + sums_ref[start : start + 8, :]
    line = jnp.sum(part, axis=0, keepdims=True)

    def entry(at):
        return jnp.sum(jnp.where(lanes(line.shape) == at, line, 0.0), axis=1, keepdims=True)

    gram = [[None] * 4 for _ in range(4)]
    at = 0
    for i in range(4):
        for j in range(i + 1):
            gram[i][j] = gram[j][i] = entry(at)
            at += 1
    tail = entry(at)

    def scaled(coef):
        out = [None] * 5
        for j, value in enumerate(coef):
            if value is None:
                continue
            moves = [(1, value)] if j == 0 else [(j + 1, 0.5 * value), (j - 1, 0.5 * value)]
            for place, amount in moves:
                out[place] = amount if out[place] is None else out[place] + amount
        return out

    def dot(left, right):
        total = None
        for i in range(4):
            for j in range(4):
                if left[i] is None or right[j] is None:
                    continue
                term = left[i] * right[j] * gram[i][j]
                total = term if total is None else total + term
        return total

    def plus(left, factor, right):
        out = []
        for a, b in zip(left, right):
            if b is None:
                out.append(a)
            elif a is None:
                out.append(factor * b)
            else:
                out.append(a + factor * b)
        return out

    one = jnp.ones_like(tail)
    residual = [one, None, None, None]
    direction = [one, None, None, None]
    solution_coef = [None] * 4
    norm = dot(residual, residual)
    for step in range(ITERS):
        moved = scaled(direction)
        if step < ITERS - 1:
            energy = dot(direction, moved[:4])
        else:
            low = direction[:3] + [None]
            moved_low = scaled(low)[:4]
            energy = (
                dot(low, moved_low)
                + 2.0 * direction[3] * dot([None, None, None, one], moved_low)
                + direction[3] * direction[3] * tail
            )
        energy = 5.0 * (energy + dot(direction, direction))
        factor = norm / energy
        solution_coef = plus(solution_coef, factor, direction)
        if step < ITERS - 1:
            image = plus([None if m is None else 5.0 * m for m in moved[:4]], 5.0, direction)
            residual = plus(residual, -factor, image)
            new = dot(residual, residual)
            direction = plus(residual, new / norm, direction)
            norm = new

    pressure = basis_ref[4]
    for j in range(4):
        pressure = pressure + solution_coef[j] * basis_ref[j]
    ocean = basis_ref[5]
    seen = ocean * pressure
    half = 0.5 * ocean
    east = half * (roll(seen, -1, 1) - roll(seen, 1, 1))
    north = half * (roll(seen, -1, 0) - roll(seen, 1, 0))
    pressure_ref[...] = pressure[0:height, 0:width]
    gradient_ref[0] = east[0:height, 0:width]
    gradient_ref[1] = north[0:height, 0:width]


def exchange(first, second, axis):
    wide, tall = lax.axis_size("gx"), lax.axis_size("gy")
    pairs, others = [], []
    for x in range(wide):
        for y in range(tall):
            at = x * tall + y
            if axis == "gx":
                pairs.append((at, (x ^ 1) * tall + y))
                others.append((at, ((x + 1 if x % 2 else x - 1) % wide) * tall + y))
            else:
                pairs.append((at, x * tall + (y ^ 1)))
                beyond = y + 1 if y % 2 else y - 1
                inside = 0 <= beyond < tall
                others.append((at, x * tall + beyond if inside else (x ^ 1) * tall + y))
    return lax.ppermute(first, AXES, pairs), lax.ppermute(second, AXES, others)


def full(shape):
    return pl.BlockSpec(shape, lambda *_: (0,) * len(shape))


def vmem():
    return pl.BlockSpec(memory_space=pltpu.VMEM)


def hbm():
    return pl.BlockSpec(memory_space=pltpu.HBM)


def smem():
    return pl.BlockSpec(memory_space=pltpu.SMEM)


def params(limit=32, **more):
    return pltpu.CompilerParams(vmem_limit_bytes=limit * MIB, **more)


def struct(*shape):
    return jax.ShapeDtypeStruct(shape, F32)


def per_device(
    tracers,
    level_counts,
    u_vel,
    v_vel,
    diff_depth,
    diff_lat,
    thickness,
    surface_forcing,
    initial_pressure,
):
    kinds, levels, height, width = tracers.shape
    packed = 2 * levels
    with jax.named_scope("pack_buoyancy"):
        buoyancy, x_first, x_second, y_first, y_second = pl.pallas_call(
            pack_buoyancy_kernel,
            in_specs=[hbm(), hbm()],
            out_shape=[
                struct(levels, height, width),
                struct(2, height, width),
                struct(2, height, width),
                struct(packed + 16, width),
                struct(packed + 16, width),
            ],
            scratch_shapes=[
                pltpu.VMEM((2, levels, height, width), F32),
                pltpu.VMEM((height, width), jnp.int32),
                pltpu.SemaphoreType.DMA((8,)),
                pltpu.SemaphoreType.DMA,
            ],
            compiler_params=params(52),
        )(tracers, level_counts)
        u_vel, v_vel, surface_forcing, initial_pressure, x_first = lax.optimization_barrier(
            (u_vel, v_vel, surface_forcing, initial_pressure, x_first)
        )
    with jax.named_scope("buoyancy_halo"):
        x_halo = exchange(x_first, x_second, "gx")
        y_halo = exchange(y_first, y_second, "gy")
    with jax.named_scope("pack_tracers"):
        early = kinds // 2
        later, _ = lax.optimization_barrier((tracers, x_first))
        packs = pack_tracers(later, 0, early)
        buoyancy, *packs = lax.optimization_barrier((buoyancy, *packs))
    with jax.named_scope("forcing"):
        fields, masks = pl.pallas_call(
            forcing_kernel,
            in_specs=[vmem()] * 4 + [smem()] * 3 + [vmem()] * 6,
            out_shape=[struct(3, height, width), struct(12, height, width)],
            scratch_shapes=[
                pltpu.VMEM((levels, height, width), F32),
                pltpu.VMEM((packed + 16, width), F32),
                pltpu.VMEM((packed + 16, width), F32),
            ],
            compiler_params=params(8),
        )(
            buoyancy,
            level_counts,
            u_vel,
            v_vel,
            diff_depth,
            diff_lat,
            thickness,
            surface_forcing,
            initial_pressure,
            *x_halo,
            *y_halo,
        )
    with jax.named_scope("fields_halo"):
        f_x_halo = exchange(fields, fields, "gx")
        later, _ = lax.optimization_barrier((tracers, fields))
        packs = pack_tracers(later, early, kinds - early, packs)
        own_fields, *packs = lax.optimization_barrier((fields, *packs))
        side, f_y_first, f_y_second = pl.pallas_call(
            outer_rows_kernel,
            out_shape=[struct(3, height, width), struct(6, 8, width), struct(6, 8, width)],
            compiler_params=params(4),
        )(own_fields, *f_x_halo)
        f_y_halo = exchange(f_y_first, f_y_second, "gy")
        masks, _ = lax.optimization_barrier((masks, f_y_first))
        side_weights = pl.pallas_call(
            side_weights_kernel,
            out_shape=struct(2, 2, height, width),
            compiler_params=params(8),
            cost_estimate=pl.CostEstimate(flops=2_000_000, bytes_accessed=2_000_000, transcendentals=0),
        )(masks, u_vel)
    with jax.named_scope("tracer_halo"):
        t_x_first, t_x_second, t_y_first, t_y_second = packs
        t_x_halo = exchange(t_x_first, t_x_second, "gx")
        *f_y_halo, t_y_first, t_y_second = lax.optimization_barrier((*f_y_halo, t_y_first, t_y_second))
        t_y_halo = exchange(t_y_first, t_y_second, "gy")
    with jax.named_scope("krylov"):
        basis, sums = pl.pallas_call(
            krylov_kernel,
            out_shape=[struct(6, height + 16, 2 * width), struct(128, width)],
            compiler_params=params(8),
        )(fields, side, *f_y_halo)
        all_sums = lax.all_to_all(sums, AXES, 0, 0, tiled=True)
    with jax.named_scope("side_terms"):
        side_weights, _ = lax.optimization_barrier((side_weights, sums))
        sides = pl.pallas_call(
            side_kernel,
            out_shape=struct(kinds, 2, height, width),
            compiler_params=params(8),
            cost_estimate=pl.CostEstimate(flops=4_000_000, bytes_accessed=3_000_000, transcendentals=0),
        )(side_weights, *t_x_halo)
    chunk = 4
    with jax.named_scope("advance"):
        new_tracers = pl.pallas_call(
            advance_kernel,
            in_specs=[hbm()] + [vmem()] * 6,
            out_specs=hbm(),
            out_shape=struct(kinds, levels, height, width),
            scratch_shapes=[
                pltpu.VMEM((kinds, levels, height, width), F32),
                pltpu.VMEM((chunk, kinds, height + 16, width), F32),
                pltpu.VMEM((chunk * kinds * height, 2 * width), jnp.bfloat16),
                pltpu.VMEM((chunk * kinds * height, 2 * width), F32),
                pltpu.VMEM((2 * width, 2 * width), jnp.bfloat16),
                pltpu.VMEM((chunk, 4, height, width), F32),
                pltpu.VMEM((kinds * packed, width), F32),
                pltpu.VMEM((kinds * packed, width), F32),
                pltpu.SemaphoreType.DMA((levels // chunk,)),
                pltpu.SemaphoreType.DMA((levels // chunk,)),
            ],
            compiler_params=params(52),
            cost_estimate=pl.CostEstimate(flops=60_000_000, bytes_accessed=22_000_000, transcendentals=0),
        )(tracers, u_vel, v_vel, masks, sides, *t_y_halo)
    with jax.named_scope("solve"):
        new_tracers, all_sums = lax.optimization_barrier((new_tracers, all_sums))
        pressure, gradient = pl.pallas_call(
            finish_kernel,
            out_shape=[struct(height, width), struct(2, height, width)],
            compiler_params=params(8),
        )(basis, all_sums)
    return new_tracers, pressure, gradient


def solution(mesh):
    return jax.shard_map(
        per_device,
        mesh=mesh,
        in_specs=(
            P(None, None, "gy", "gx"),
            P("gy", "gx"),
            P(None, "gy", "gx"),
            P(None, "gy", "gx"),
            P(),
            P("gy"),
            P(),
            P("gy", "gx"),
            P("gy", "gx"),
        ),
        out_specs=(P(None, None, "gy", "gx"), P("gy", "gx"), P(None, "gy", "gx")),
        check_vma=False,
    )
```

```python
import functools

import jax
import jax.numpy as jnp
from jax import lax
from jax.experimental import pallas as pl
from jax.experimental.pallas import tpu as pltpu
from jax.sharding import PartitionSpec as P

ITERS = 4
F32 = jnp.float32
AXES = ("gx", "gy")
MIB = 1024 * 1024


def roll(values, shift, axis):
    size = values.shape[axis]
    if isinstance(shift, int):
        shift = shift % size
        if shift == 0:
            return values
    return pltpu.roll(values, shift, axis)


def lanes(shape):
    return lax.broadcasted_iota(jnp.int32, shape, len(shape) - 1)


def rows(shape):
    return lax.broadcasted_iota(jnp.int32, shape, len(shape) - 2)


def pack_columns(load, levels):
    half = levels // 2
    groups = []
    for group in range(2):
        packed = None
        for at in range(half):
            values = load(group * half + at)
            moved = roll(values, 4 * at - 126, 1)
            if packed is None:
                packed = moved
            else:
                packed = jnp.where(lanes(moved.shape) // 4 == at, moved, packed)
        groups.append(packed)
    low = lanes(groups[0].shape) % 4 < 2
    last = jnp.where(low, groups[0], roll(groups[1], 2, 1))
    first = jnp.where(low, roll(groups[0], -2, 1), groups[1])
    return last, first


def unpack_groups(from_west, from_east):
    low = lanes(from_west.shape) % 4 < 2
    return (
        jnp.where(low, from_west, roll(from_east, 2, 1)),
        jnp.where(low, roll(from_west, -2, 1), from_east),
    )


def is_even(axis):
    return lax.axis_index(axis) % 2 == 0


def copy_in(source, place, semaphore, parts):
    copies = []
    size = source.shape[0] // parts
    for part in range(parts):
        where = pl.ds(part * size, size)
        copies.append(pltpu.make_async_copy(source.at[where], place.at[where], semaphore.at[part]))
        copies[-1].start()
    return copies


def pack_buoyancy_kernel(
    tracers_ref,
    counts_ref,
    b_ref,
    x_first_ref,
    x_second_ref,
    y_first_ref,
    y_second_ref,
    held,
    counts_s,
    semaphore,
    counts_semaphore,
):
    levels, height = b_ref.shape[0], b_ref.shape[1]
    parts = semaphore.shape[0] // 2
    warm = copy_in(tracers_ref.at[0], held.at[0], semaphore.at[pl.ds(0, parts)], parts)
    salt = copy_in(tracers_ref.at[1], held.at[1], semaphore.at[pl.ds(parts, parts)], parts)
    counts_copy = pltpu.make_async_copy(counts_ref, counts_s, counts_semaphore)
    counts_copy.start()
    even_x, even_y = is_even("gx"), is_even("gy")

    def load(level):
        if level % (levels // parts) == 0:
            warm[level // (levels // parts)].wait()
            salt[level // (levels // parts)].wait()
        values = 0.2 * held[0, level] - 0.8 * held[1, level]
        b_ref[level] = values
        high, low = values[height - 2 : height, :], values[0:2, :]
        y_first_ref[8 + 2 * level : 10 + 2 * level, :] = jnp.where(even_y, high, low)
        y_second_ref[8 + 2 * level : 10 + 2 * level, :] = jnp.where(even_y, low, high)
        return values

    last, first = pack_columns(load, levels)
    x_first_ref[0] = jnp.where(even_x, last, first)
    x_second_ref[0] = jnp.where(even_x, first, last)
    counts_copy.wait()
    counts = counts_s[...].astype(F32)
    x_first_ref[1] = counts
    x_second_ref[1] = counts
    low, high = counts[0:8, :], counts[height - 8 : height, :]
    for start in (0, 8 + 2 * levels):
        y_first_ref[start : start + 8, :] = jnp.where(even_y, high, low)
        y_second_ref[start : start + 8, :] = jnp.where(even_y, low, high)


def pack_tracers_kernel(first_kind, tracers_ref, *refs):
    x_first_ref, x_second_ref, y_first_ref, y_second_ref = refs[-4:]
    total, levels, height, width = tracers_ref.shape
    kinds = x_first_ref.shape[0] - first_kind
    even_x, even_y = is_even("gx"), is_even("gy")

    flat = tracers_ref.reshape(total * levels * height, width)
    for before_ref, ref in zip(refs[:-4], refs[-4:]):
        ref[0:first_kind] = before_ref[...]

    def one_kind(kind, carry):
        place = first_kind + kind

        for side_row in range(2):
            for start in range(0, levels - 8, 8):
                base = (place * levels + start) * height + side_row
                high = flat[pl.ds(base + height - 2, 8, stride=height), :]
                low = flat[pl.ds(base, 8, stride=height), :]
                tile = pl.ds(side_row * levels + start, 8)
                y_first_ref[place, tile, :] = jnp.where(even_y, high, low)
                y_second_ref[place, tile, :] = jnp.where(even_y, low, high)
        for level in range(levels - 8, levels):
            for side_row in range(2):
                at = height - 2 + side_row
                high = tracers_ref[place, level, at : at + 1, :]
                low = tracers_ref[place, level, side_row : side_row + 1, :]
                into = side_row * levels + level
                y_first_ref[place, into : into + 1, :] = jnp.where(even_y, high, low)
                y_second_ref[place, into : into + 1, :] = jnp.where(even_y, low, high)
        last, first = pack_columns(lambda level: tracers_ref[place, level], levels)
        x_first_ref[place] = jnp.where(even_x, last, first)
        x_second_ref[place] = jnp.where(even_x, first, last)
        return carry

    lax.fori_loop(0, kinds, one_kind, 0)


def pack_tracers(tracers, first_kind, count, before=()):
    kinds, levels, height, width = tracers.shape
    upto = first_kind + count
    return pl.pallas_call(
        functools.partial(pack_tracers_kernel, first_kind),
        in_specs=[vmem()] * (1 + len(before)),
        out_shape=[struct(upto, height, width)] * 2 + [struct(upto, 2 * levels, width)] * 2,
        compiler_params=params(20),
        cost_estimate=pl.CostEstimate(flops=10_000_000, bytes_accessed=6_000_000, transcendentals=0),
    )(tracers, *before)


def weights_of(level, mixing, tile, masks_ref, u, v):
    u8, u1 = u * (8.0 / 12.0), u * (1.0 / 12.0)
    v8, v1 = v * (8.0 / 12.0), v * (1.0 / 12.0)
    plain = (mixing - u8, mixing + u8, u1, -u1, mixing - v8, mixing + v8, v1, -v1)
    height = level.astype(F32)
    out = [jnp.where(height < masks_ref[at, tile, :], plain[at], 0.0) for at in range(8)]
    total = out[0]
    for weight in out[1:]:
        total = total + weight
    return out, 1.0 - total


def stencil(weights, own, tile_at, tiles, load_at, side, north_1, north_2, south_1, south_2):
    column = lanes(own.shape)
    row = rows(own.shape)
    base = 8 * tile_at
    width = own.shape[1]
    if tile_at + 1 < tiles:
        n1, n2 = load_at(base + 1), load_at(base + 2)
    else:
        n1 = jnp.where(row == 7, north_1(), roll(own, -1, 0))
        n2 = jnp.where(row >= 6, north_2(), roll(own, -2, 0))
    if tile_at > 0:
        s1, s2 = load_at(base - 1), load_at(base - 2)
    else:
        s1 = jnp.where(row == 0, south_1(), roll(own, 1, 0))
        s2 = jnp.where(row < 2, south_2(), roll(own, 2, 0))
    near, middle = weights
    total = middle * own
    for weight, value in zip(
        near,
        (
            roll(jnp.where(column < 1, side, own), -1, 1),
            roll(jnp.where(column >= width - 1, side, own), 1, 1),
            roll(jnp.where(column < 2, side, own), -2, 1),
            roll(jnp.where(column >= width - 2, side, own), 2, 1),
            n1,
            s1,
            n2,
            s2,
        ),
    ):
        total = total + weight * value
    return total


def table_parts(tables_ref, levels):
    planes, height, width = tables_ref.shape
    flat = tables_ref.reshape(planes * height, width)
    start = 9 * height
    return flat.at[pl.ds(start, height + 16)], flat.at[pl.ds(start + height + 16, levels)]


def forcing_kernel(
    b_ref,
    counts_ref,
    u_ref,
    v_ref,
    depth_ref,
    lat_ref,
    thick_ref,
    surface_ref,
    pressure_ref,
    x_first_ref,
    x_second_ref,
    y_first_ref,
    y_second_ref,
    fields_ref,
    masks_ref,
    sides_s,
    north_s,
    south_s,
):
    levels, height, width = b_ref.shape
    tiles = height // 8
    half = levels // 2
    counts_s, depths_ref = table_parts(masks_ref, levels)
    gx, gy = lax.axis_index("gx"), lax.axis_index("gy")
    even_x, even_y = is_even("gx"), is_even("gy")
    end_x, end_y = lax.axis_size("gx") - 1, lax.axis_size("gy") - 1
    counts = counts_ref[...].astype(F32)
    column = lanes(counts.shape)
    east = jnp.where(even_x, x_first_ref[1], x_second_ref[1]) * jnp.where(gx < end_x, 1.0, 0.0)
    west = jnp.where(even_x, x_second_ref[1], x_first_ref[1]) * jnp.where(gx > 0, 1.0, 0.0)
    north_s[...] = jnp.where(even_y, y_first_ref[...], y_second_ref[...])
    south_s[...] = jnp.where(even_y, y_second_ref[...], y_first_ref[...])
    masks_ref[0] = jnp.minimum(counts, roll(jnp.where(column < 1, east, counts), -1, 1))
    masks_ref[1] = jnp.minimum(counts, roll(jnp.where(column >= width - 1, west, counts), 1, 1))
    masks_ref[2] = jnp.minimum(counts, roll(jnp.where(column < 2, east, counts), -2, 1))
    masks_ref[3] = jnp.minimum(counts, roll(jnp.where(column >= width - 2, west, counts), 2, 1))
    counts_s[0:8, :] = south_s[0:8, :] * jnp.where(gy > 0, 1.0, 0.0)
    counts_s[8 : 8 + height, :] = counts
    counts_s[8 + height : 16 + height, :] = north_s[0:8, :] * jnp.where(gy < end_y, 1.0, 0.0)
    masks_ref[4] = jnp.minimum(counts, counts_s[9 : 9 + height, :])
    masks_ref[5] = jnp.minimum(counts, counts_s[7 : 7 + height, :])
    masks_ref[6] = jnp.minimum(counts, counts_s[10 : 10 + height, :])
    masks_ref[7] = jnp.minimum(counts, counts_s[6 : 6 + height, :])
    for level in range(levels):
        depths_ref[level : level + 1, :] = jnp.full((1, width), depth_ref[level], F32)
    row = rows(counts.shape)
    lat = jnp.zeros(counts.shape, F32)
    for at in range(height):
        lat = jnp.where(row == at, lat_ref[at], lat)
    masks_ref[8] = lat
    groups = unpack_groups(
        jnp.where(even_x, x_second_ref[0], x_first_ref[0]), jnp.where(even_x, x_first_ref[0], x_second_ref[0])
    )
    for level in range(levels):
        sides_s[level] = roll(groups[level // half], 126 - 4 * (level % half), 1)

    def level_body(level, carry):
        thick = thick_ref[level]
        forcing, depth_sum = list(carry[0]), list(carry[1])
        for tile_at in range(tiles):
            tile = pl.ds(8 * tile_at, 8)
            mixing = depth_ref[level] * masks_ref[8, tile, :]
            weights = weights_of(level, mixing, tile, masks_ref, u_ref[level, tile, :], v_ref[level, tile, :])
            value = stencil(
                weights,
                b_ref[level, tile, :],
                tile_at,
                tiles,
                lambda start: b_ref[level, pl.ds(start, 8), :],
                sides_s[level, tile, :],
                lambda: north_s[pl.ds(2 * level + 1, 8), :],
                lambda: north_s[pl.ds(2 * level + 2, 8), :],
                lambda: south_s[pl.ds(2 * level + 9, 8), :],
                lambda: south_s[pl.ds(2 * level + 8, 8), :],
            )
            weight = jnp.where(level.astype(F32) < counts_s[pl.ds(8 + 8 * tile_at, 8), :], thick, 0.0)
            forcing[tile_at] = forcing[tile_at] + weight * value
            depth_sum[tile_at] = depth_sum[tile_at] + weight
        return tuple(forcing), tuple(depth_sum)

    zeros = tuple(jnp.zeros((8, width), F32) for _ in range(tiles))
    forcing, depth_sum = lax.fori_loop(0, levels, level_body, (zeros, zeros), unroll=4)
    for at in range(tiles):
        tile = pl.ds(8 * at, 8)
        ocean = jnp.where(counts_s[pl.ds(8 + 8 * at, 8), :] > 0.0, 1.0, 0.0)
        fields_ref[0, tile, :] = ocean * (0.5 * forcing[at] + surface_ref[tile, :])
        fields_ref[1, tile, :] = pressure_ref[tile, :]
        fields_ref[2, tile, :] = 5.0 + 2.0 / (1.0 + depth_sum[at])


def shift_matrix():
    shape = (256, 256)
    column = lanes(shape)
    offset = rows(shape) % 128 - column % 128
    near = jnp.where(offset == 1, 1.0, 0.0)
    far = jnp.where(offset == -1, 1.0, 0.0)
    both = jnp.where(offset == 2, 1.0, 0.0) - jnp.where(offset == -2, 1.0, 0.0)
    return jnp.where(column < 128, near + far, 8.0 * (near - far) - both).astype(jnp.bfloat16)


def side_weights_kernel(masks_ref, u_ref, weights_ref):
    levels, height, width = u_ref.shape
    half = levels // 2
    depths_ref = table_parts(masks_ref, levels)[1]
    column = lanes((height, width))
    for group in range(2):
        near, far = jnp.zeros((height, width), F32), jnp.zeros((height, width), F32)
        for at in range(half):
            level = group * half + at
            mixing = depths_ref[level : level + 1, :] * masks_ref[8]
            u8, u1 = u_ref[level] * (8.0 / 12.0), u_ref[level] * (1.0 / 12.0)
            first = jnp.where(
                column == width - 1,
                jnp.where(level < masks_ref[0], mixing - u8, 0.0),
                jnp.where(level < masks_ref[1], mixing + u8, 0.0),
            )
            first = jnp.where((column == 0) | (column == width - 1), first, 0.0)
            second = jnp.where(
                column < 2, jnp.where(level < masks_ref[3], -u1, 0.0), jnp.where(level < masks_ref[2], u1, 0.0)
            )
            here = column // 4 == at
            near = jnp.where(here, roll(first, 4 * at - 126, 1), near)
            far = jnp.where(here, roll(second, 4 * at - 126, 1), far)
        weights_ref[group, 0] = near
        weights_ref[group, 1] = far


def side_kernel(weights_ref, x_first_ref, x_second_ref, sides_ref):
    kinds, height, width = x_first_ref.shape
    even_x = is_even("gx")
    spot = lanes((height, width)) % 4
    for kind in range(kinds):
        x_first, x_second = x_first_ref[kind], x_second_ref[kind]
        groups = unpack_groups(jnp.where(even_x, x_second, x_first), jnp.where(even_x, x_first, x_second))
        for group, values in enumerate(groups):
            by_two = jnp.where(spot < 2, roll(values, -2, 1), roll(values, 2, 1))
            by_one = jnp.where(spot < 2, roll(values, -1, 1), roll(values, 1, 1))
            sides_ref[kind, group] = weights_ref[group, 0] * by_one + weights_ref[group, 1] * by_two


def advance_kernel(
    tracers_ref,
    u_ref,
    v_ref,
    masks_ref,
    sides_ref,
    y_first_ref,
    y_second_ref,
    out_ref,
    held,
    masked_s,
    parts_s,
    moved_s,
    matrix_s,
    weights_s,
    north_s,
    south_s,
    in_semaphore,
    out_semaphore,
):
    kinds, levels, height, width = tracers_ref.shape
    groups = in_semaphore.shape[0]
    chunk = levels // groups
    tiles = height // 8
    half = levels // 2
    counts_ref, depths_ref = table_parts(masks_ref, levels)

    def load(group):
        where = (slice(None), pl.ds(group * chunk, chunk))
        return pltpu.make_async_copy(tracers_ref.at[where], held.at[where], in_semaphore.at[group])

    def store(group):
        where = (slice(None), pl.ds(group * chunk, chunk))
        return pltpu.make_async_copy(held.at[where], out_ref.at[where], out_semaphore.at[group])

    for group in range(groups):
        load(group).start()
    matrix_s[...] = shift_matrix()
    even_y = is_even("gy")
    for side_row in range(2):
        south_counts = counts_ref[6 + side_row : 7 + side_row, :]
        north_counts = counts_ref[8 + height + side_row : 9 + height + side_row, :]
        for start in range(0, levels, 8):
            number = (rows((8, width)) + start).astype(F32)
            in_north, in_south = number < north_counts, number < south_counts
            tile = pl.ds(side_row * levels + start, 8)
            for kind in range(kinds):
                first, second = y_first_ref[kind, tile, :], y_second_ref[kind, tile, :]
                into = pl.ds(2 * (kind * levels + start) + side_row, 8, stride=2)
                north_s[into, :] = jnp.where(in_north, jnp.where(even_y, first, second), 0.0)
                south_s[into, :] = jnp.where(in_south, jnp.where(even_y, second, first), 0.0)
    column = lanes((8, width))
    outer = (column < 2) | (column >= width - 2)

    def prepare(level, at):
        number = level.astype(F32)
        for tile_at in range(tiles):
            tile = pl.ds(8 * tile_at, 8)
            mixing = depths_ref[pl.ds(level, 1), :] * masks_ref[8, tile, :]
            u, v = u_ref[level, tile, :], v_ref[level, tile, :]
            active = number < counts_ref[pl.ds(8 + 8 * tile_at, 8), :]
            weights_s[at, 0, tile, :] = weights_of(level, mixing, tile, masks_ref, u, v)[1]
            weights_s[at, 1, tile, :] = jnp.where(active, mixing, 0.0)
            weights_s[at, 2, tile, :] = jnp.where(active, u * (-1.0 / 12.0), 0.0)
            weights_s[at, 3, tile, :] = jnp.where(active, v * (-1.0 / 12.0), 0.0)
        active = number < counts_ref[8 : 8 + height, :]
        for kind in range(kinds):
            seen = jnp.where(active, held[kind, level], 0.0)
            masked_s[at, kind, 8 : 8 + height, :] = seen
            high = seen.astype(jnp.bfloat16)
            row = (at * kinds + kind) * height
            parts_s[row : row + height, 0:width] = high
            parts_s[row : row + height, width : 2 * width] = (seen - high.astype(F32)).astype(jnp.bfloat16)
            masked_s[at, kind, 8 + height : 10 + height, :] = north_s[pl.ds(2 * (kind * levels + level), 2), :]
            masked_s[at, kind, 6:8, :] = south_s[pl.ds(2 * (kind * levels + level), 2), :]

    def finish(level, at):
        group = level // half
        shift = 126 - 4 * (level - half * group)
        for tile_at in range(tiles):
            base = 8 * tile_at
            tile = pl.ds(base, 8)
            own_weight, mixing, eastward, northward = (weights_s[at, i, tile, :] for i in range(4))
            for kind in range(kinds):
                row = (at * kinds + kind) * height + base
                n1, s1, n2, s2 = (masked_s[at, kind, pl.ds(8 + base + by, 8), :] for by in (1, -1, 2, -2))
                side = jnp.where(outer, pltpu.roll(sides_ref[kind, group, tile, :], shift, 1), 0.0)
                held[kind, level, tile, :] = (
                    own_weight * held[kind, level, tile, :]
                    + mixing * (moved_s[row : row + 8, 0:width] + (n1 + s1))
                    + eastward * moved_s[row : row + 8, width : 2 * width]
                    + northward * (8.0 * (n1 - s1) - (n2 - s2))
                    + side
                )

    def one_group(group, carry):
        load(group).wait()
        for at in range(chunk):
            prepare(group * chunk + at, at)
        moved_s[...] = jnp.dot(parts_s[...], matrix_s[...], preferred_element_type=F32)
        for at in range(chunk):
            finish(group * chunk + at, at)
        store(group).start()
        return carry

    lax.fori_loop(0, groups, one_group, 0)
    for group in range(groups):
        store(group).wait()


def outer_rows_kernel(fields_ref, x_first_ref, x_second_ref, side_ref, y_first_ref, y_second_ref):
    count, height, width = fields_ref.shape
    even_x, even_y = is_even("gx"), is_even("gy")
    eastern = (lanes((height, width)) < width // 2) == even_x
    for at in range(count):
        side = jnp.where(eastern, x_first_ref[at], x_second_ref[at])
        side_ref[at] = side
        for place, values in ((at, fields_ref[at]), (count + at, side)):
            low, high = values[0:8, :], values[height - 8 : height, :]
            y_first_ref[place] = jnp.where(even_y, high, low)
            y_second_ref[place] = jnp.where(even_y, low, high)


def extended(fields_ref, side_ref, y_first_ref, y_second_ref, at):
    count = fields_ref.shape[0]
    even_y = is_even("gy")

    def column(inner, place):
        first, second = y_first_ref[place], y_second_ref[place]
        return jnp.concatenate([inner, jnp.where(even_y, first, second), jnp.where(even_y, second, first)], axis=0)

    return jnp.concatenate([column(fields_ref[at], at), column(side_ref[at], count + at)], axis=1)


def krylov_kernel(fields_ref, side_ref, y_first_ref, y_second_ref, basis_ref, sums_ref):
    height, width = fields_ref.shape[1], fields_ref.shape[2]
    forcing, pressure, center = (
        extended(fields_ref, side_ref, y_first_ref, y_second_ref, at) for at in range(3)
    )
    shape = forcing.shape
    column, row = lanes(shape), rows(shape)
    gx, gy = lax.axis_index("gx"), lax.axis_index("gy")
    end_x, end_y = lax.axis_size("gx") - 1, lax.axis_size("gy") - 1
    least_column = jnp.where(gx < end_x, 0, width)
    most_column = jnp.where(gx > 0, 2 * width, width + width // 2)
    least_row = jnp.where(gy < end_y, 0, height)
    most_row = jnp.where(gy > 0, height + 16, height + 8)
    inside_x = (column < width) | ((column >= least_column) & (column < width + width // 2) & (gx < end_x)) | (
        (column >= width + width // 2) & (column < most_column)
    )
    inside_y = (row < height) | ((row >= least_row) & (row < height + 8) & (gy < end_y)) | (
        (row >= height + 8) & (row < most_row)
    )
    ocean = jnp.where((center < 6.75) & inside_x & inside_y, 1.0, 0.0)
    diagonal = jnp.where(ocean > 0.0, center, 1.0)

    def operate(values):
        seen = ocean * values
        beside = roll(seen, 1, 1) + roll(seen, -1, 1)
        mixed = seen + 0.25 * beside
        return diagonal * values - ocean * (beside + (roll(mixed, 1, 0) + roll(mixed, -1, 0)))

    def scaled(values):
        return 0.2 * operate(values) - values

    base = [forcing - operate(pressure)]
    base.append(scaled(base[0]))
    base.append(2.0 * scaled(base[1]) - base[0])
    base.append(2.0 * scaled(base[2]) - base[1])
    last = scaled(base[3])
    for at in range(4):
        basis_ref[at] = base[at]
    basis_ref[4] = pressure
    basis_ref[5] = ocean
    inner = [values[0:height, 0:width] for values in base]
    sums = []
    for at in range(4):
        for other in range(at + 1):
            sums.append(inner[at] * inner[other])
    sums.append(inner[3] * last[0:height, 0:width])
    line = jnp.zeros((8, width), F32)
    for at, values in enumerate(sums):
        part = values[0:8]
        for start in range(8, height, 8):
            part = part + values[start : start + 8]
        total = jnp.sum(jnp.sum(part, axis=0, keepdims=True), axis=1, keepdims=True)
        line = jnp.where(lanes(line.shape) == at, total, line)
    for start in range(0, sums_ref.shape[0], 8):
        sums_ref[start : start + 8, :] = line


def finish_kernel(basis_ref, sums_ref, pressure_ref, gradient_ref):
    height, width = pressure_ref.shape
    part = sums_ref[0:8, :]
    for start in range(8, sums_ref.shape[0], 8):
        part = part + sums_ref[start : start + 8, :]
    line = jnp.sum(part, axis=0, keepdims=True)

    def entry(at):
        return jnp.sum(jnp.where(lanes(line.shape) == at, line, 0.0), axis=1, keepdims=True)

    gram = [[None] * 4 for _ in range(4)]
    at = 0
    for i in range(4):
        for j in range(i + 1):
            gram[i][j] = gram[j][i] = entry(at)
            at += 1
    tail = entry(at)

    def scaled(coef):
        out = [None] * 5
        for j, value in enumerate(coef):
            if value is None:
                continue
            moves = [(1, value)] if j == 0 else [(j + 1, 0.5 * value), (j - 1, 0.5 * value)]
            for place, amount in moves:
                out[place] = amount if out[place] is None else out[place] + amount
        return out

    def dot(left, right):
        total = None
        for i in range(4):
            for j in range(4):
                if left[i] is None or right[j] is None:
                    continue
                term = left[i] * right[j] * gram[i][j]
                total = term if total is None else total + term
        return total

    def plus(left, factor, right):
        out = []
        for a, b in zip(left, right):
            if b is None:
                out.append(a)
            elif a is None:
                out.append(factor * b)
            else:
                out.append(a + factor * b)
        return out

    one = jnp.ones_like(tail)
    residual = [one, None, None, None]
    direction = [one, None, None, None]
    solution_coef = [None] * 4
    norm = dot(residual, residual)
    for step in range(ITERS):
        moved = scaled(direction)
        if step < ITERS - 1:
            energy = dot(direction, moved[:4])
        else:
            low = direction[:3] + [None]
            moved_low = scaled(low)[:4]
            energy = (
                dot(low, moved_low)
                + 2.0 * direction[3] * dot([None, None, None, one], moved_low)
                + direction[3] * direction[3] * tail
            )
        energy = 5.0 * (energy + dot(direction, direction))
        factor = norm / energy
        solution_coef = plus(solution_coef, factor, direction)
        if step < ITERS - 1:
            image = plus([None if m is None else 5.0 * m for m in moved[:4]], 5.0, direction)
            residual = plus(residual, -factor, image)
            new = dot(residual, residual)
            direction = plus(residual, new / norm, direction)
            norm = new

    pressure = basis_ref[4]
    for j in range(4):
        pressure = pressure + solution_coef[j] * basis_ref[j]
    ocean = basis_ref[5]
    seen = ocean * pressure
    half = 0.5 * ocean
    east = half * (roll(seen, -1, 1) - roll(seen, 1, 1))
    north = half * (roll(seen, -1, 0) - roll(seen, 1, 0))
    pressure_ref[...] = pressure[0:height, 0:width]
    gradient_ref[0] = east[0:height, 0:width]
    gradient_ref[1] = north[0:height, 0:width]


def exchange(first, second, axis):
    wide, tall = lax.axis_size("gx"), lax.axis_size("gy")
    pairs, others = [], []
    for x in range(wide):
        for y in range(tall):
            at = x * tall + y
            if axis == "gx":
                pairs.append((at, (x ^ 1) * tall + y))
                others.append((at, ((x + 1 if x % 2 else x - 1) % wide) * tall + y))
            else:
                pairs.append((at, x * tall + (y ^ 1)))
                beyond = y + 1 if y % 2 else y - 1
                inside = 0 <= beyond < tall
                others.append((at, x * tall + beyond if inside else (x ^ 1) * tall + y))
    return lax.ppermute(first, AXES, pairs), lax.ppermute(second, AXES, others)


def full(shape):
    return pl.BlockSpec(shape, lambda *_: (0,) * len(shape))


def vmem():
    return pl.BlockSpec(memory_space=pltpu.VMEM)


def hbm():
    return pl.BlockSpec(memory_space=pltpu.HBM)


def smem():
    return pl.BlockSpec(memory_space=pltpu.SMEM)


def params(limit=32, **more):
    return pltpu.CompilerParams(vmem_limit_bytes=limit * MIB, **more)


def struct(*shape):
    return jax.ShapeDtypeStruct(shape, F32)


def per_device(
    tracers,
    level_counts,
    u_vel,
    v_vel,
    diff_depth,
    diff_lat,
    thickness,
    surface_forcing,
    initial_pressure,
):
    kinds, levels, height, width = tracers.shape
    packed = 2 * levels
    with jax.named_scope("pack_buoyancy"):
        buoyancy, x_first, x_second, y_first, y_second = pl.pallas_call(
            pack_buoyancy_kernel,
            in_specs=[hbm(), hbm()],
            out_shape=[
                struct(levels, height, width),
                struct(2, height, width),
                struct(2, height, width),
                struct(packed + 16, width),
                struct(packed + 16, width),
            ],
            scratch_shapes=[
                pltpu.VMEM((2, levels, height, width), F32),
                pltpu.VMEM((height, width), jnp.int32),
                pltpu.SemaphoreType.DMA((8,)),
                pltpu.SemaphoreType.DMA,
            ],
            compiler_params=params(52),
        )(tracers, level_counts)
        u_vel, v_vel, surface_forcing, initial_pressure, x_first = lax.optimization_barrier(
            (u_vel, v_vel, surface_forcing, initial_pressure, x_first)
        )
    with jax.named_scope("buoyancy_halo"):
        x_halo = exchange(x_first, x_second, "gx")
        y_halo = exchange(y_first, y_second, "gy")
    with jax.named_scope("pack_tracers"):
        early = kinds // 2
        later, _ = lax.optimization_barrier((tracers, x_first))
        packs = pack_tracers(later, 0, early)
        buoyancy, *packs = lax.optimization_barrier((buoyancy, *packs))
    with jax.named_scope("forcing"):
        fields, masks = pl.pallas_call(
            forcing_kernel,
            in_specs=[vmem()] * 4 + [smem()] * 3 + [vmem()] * 6,
            out_shape=[struct(3, height, width), struct(12, height, width)],
            scratch_shapes=[
                pltpu.VMEM((levels, height, width), F32),
                pltpu.VMEM((packed + 16, width), F32),
                pltpu.VMEM((packed + 16, width), F32),
            ],
            compiler_params=params(8),
        )(
            buoyancy,
            level_counts,
            u_vel,
            v_vel,
            diff_depth,
            diff_lat,
            thickness,
            surface_forcing,
            initial_pressure,
            *x_halo,
            *y_halo,
        )
    with jax.named_scope("fields_halo"):
        f_x_halo = exchange(fields, fields, "gx")
        later, _ = lax.optimization_barrier((tracers, fields))
        packs = pack_tracers(later, early, kinds - early, packs)
        own_fields, *packs = lax.optimization_barrier((fields, *packs))
        side, f_y_first, f_y_second = pl.pallas_call(
            outer_rows_kernel,
            out_shape=[struct(3, height, width), struct(6, 8, width), struct(6, 8, width)],
            compiler_params=params(4),
        )(own_fields, *f_x_halo)
        f_y_halo = exchange(f_y_first, f_y_second, "gy")
        masks, _ = lax.optimization_barrier((masks, f_y_first))
        side_weights = pl.pallas_call(
            side_weights_kernel,
            out_shape=struct(2, 2, height, width),
            compiler_params=params(8),
            cost_estimate=pl.CostEstimate(flops=2_000_000, bytes_accessed=2_000_000, transcendentals=0),
        )(masks, u_vel)
    with jax.named_scope("tracer_halo"):
        t_x_first, t_x_second, t_y_first, t_y_second = packs
        t_x_halo = exchange(t_x_first, t_x_second, "gx")
        *f_y_halo, t_y_first, t_y_second = lax.optimization_barrier((*f_y_halo, t_y_first, t_y_second))
        t_y_halo = exchange(t_y_first, t_y_second, "gy")
    with jax.named_scope("krylov"):
        basis, sums = pl.pallas_call(
            krylov_kernel,
            out_shape=[struct(6, height + 16, 2 * width), struct(128, width)],
            compiler_params=params(8),
        )(fields, side, *f_y_halo)
        all_sums = lax.all_to_all(sums, AXES, 0, 0, tiled=True)
    with jax.named_scope("side_terms"):
        side_weights, _ = lax.optimization_barrier((side_weights, sums))
        sides = pl.pallas_call(
            side_kernel,
            out_shape=struct(kinds, 2, height, width),
            compiler_params=params(8),
            cost_estimate=pl.CostEstimate(flops=4_000_000, bytes_accessed=3_000_000, transcendentals=0),
        )(side_weights, *t_x_halo)
    with jax.named_scope("solve"):
        sides, all_sums = lax.optimization_barrier((sides, all_sums))
        pressure, gradient = pl.pallas_call(
            finish_kernel,
            out_shape=[struct(height, width), struct(2, height, width)],
            compiler_params=params(8),
        )(basis, all_sums)
        sides, pressure = lax.optimization_barrier((sides, pressure))
    chunk = 4
    with jax.named_scope("advance"):
        new_tracers = pl.pallas_call(
            advance_kernel,
            in_specs=[hbm()] + [vmem()] * 6,
            out_specs=hbm(),
            out_shape=struct(kinds, levels, height, width),
            scratch_shapes=[
                pltpu.VMEM((kinds, levels, height, width), F32),
                pltpu.VMEM((chunk, kinds, height + 16, width), F32),
                pltpu.VMEM((chunk * kinds * height, 2 * width), jnp.bfloat16),
                pltpu.VMEM((chunk * kinds * height, 2 * width), F32),
                pltpu.VMEM((2 * width, 2 * width), jnp.bfloat16),
                pltpu.VMEM((chunk, 4, height, width), F32),
                pltpu.VMEM((kinds * packed + 8, width), F32),
                pltpu.VMEM((kinds * packed + 8, width), F32),
                pltpu.SemaphoreType.DMA((levels // chunk,)),
                pltpu.SemaphoreType.DMA((levels // chunk,)),
            ],
            compiler_params=params(52),
            cost_estimate=pl.CostEstimate(flops=60_000_000, bytes_accessed=22_000_000, transcendentals=0),
        )(tracers, u_vel, v_vel, masks, sides, *t_y_halo)
    return new_tracers, pressure, gradient


def solution(mesh):
    return jax.shard_map(
        per_device,
        mesh=mesh,
        in_specs=(
            P(None, None, "gy", "gx"),
            P("gy", "gx"),
            P(None, "gy", "gx"),
            P(None, "gy", "gx"),
            P(),
            P("gy"),
            P(),
            P("gy", "gx"),
            P("gy", "gx"),
        ),
        out_specs=(P(None, None, "gy", "gx"), P("gy", "gx"), P(None, "gy", "gx")),
        check_vma=False,
    )
```

```python
import functools

import jax
import jax.numpy as jnp
from jax import lax
from jax.experimental import pallas as pl
from jax.experimental.pallas import tpu as pltpu
from jax.sharding import PartitionSpec as P

ITERS = 4
F32 = jnp.float32
AXES = ("gx", "gy")
MIB = 1024 * 1024


def roll(values, shift, axis):
    size = values.shape[axis]
    if isinstance(shift, int):
        shift = shift % size
        if shift == 0:
            return values
    return pltpu.roll(values, shift, axis)


def lanes(shape):
    return lax.broadcasted_iota(jnp.int32, shape, len(shape) - 1)


def rows(shape):
    return lax.broadcasted_iota(jnp.int32, shape, len(shape) - 2)


def pack_columns(load, levels):
    half = levels // 2
    groups = []
    for group in range(2):
        packed = None
        for at in range(half):
            values = load(group * half + at)
            moved = roll(values, 4 * at - 126, 1)
            if packed is None:
                packed = moved
            else:
                packed = jnp.where(lanes(moved.shape) // 4 == at, moved, packed)
        groups.append(packed)
    low = lanes(groups[0].shape) % 4 < 2
    last = jnp.where(low, groups[0], roll(groups[1], 2, 1))
    first = jnp.where(low, roll(groups[0], -2, 1), groups[1])
    return last, first


def unpack_groups(from_west, from_east):
    low = lanes(from_west.shape) % 4 < 2
    return (
        jnp.where(low, from_west, roll(from_east, 2, 1)),
        jnp.where(low, roll(from_west, -2, 1), from_east),
    )


def is_even(axis):
    return lax.axis_index(axis) % 2 == 0


def copy_in(source, place, semaphore, parts):
    copies = []
    size = source.shape[0] // parts
    for part in range(parts):
        where = pl.ds(part * size, size)
        copies.append(pltpu.make_async_copy(source.at[where], place.at[where], semaphore.at[part]))
        copies[-1].start()
    return copies


def pack_buoyancy_kernel(
    tracers_ref,
    counts_ref,
    b_ref,
    x_first_ref,
    x_second_ref,
    y_first_ref,
    y_second_ref,
    held,
    counts_s,
    semaphore,
    counts_semaphore,
):
    levels, height = b_ref.shape[0], b_ref.shape[1]
    parts = semaphore.shape[0] // 2
    warm = copy_in(tracers_ref.at[0], held.at[0], semaphore.at[pl.ds(0, parts)], parts)
    salt = copy_in(tracers_ref.at[1], held.at[1], semaphore.at[pl.ds(parts, parts)], parts)
    counts_copy = pltpu.make_async_copy(counts_ref, counts_s, counts_semaphore)
    counts_copy.start()
    even_x, even_y = is_even("gx"), is_even("gy")

    def load(level):
        if level % (levels // parts) == 0:
            warm[level // (levels // parts)].wait()
            salt[level // (levels // parts)].wait()
        values = 0.2 * held[0, level] - 0.8 * held[1, level]
        b_ref[level] = values
        high, low = values[height - 2 : height, :], values[0:2, :]
        y_first_ref[8 + 2 * level : 10 + 2 * level, :] = jnp.where(even_y, high, low)
        y_second_ref[8 + 2 * level : 10 + 2 * level, :] = jnp.where(even_y, low, high)
        return values

    last, first = pack_columns(load, levels)
    x_first_ref[0] = jnp.where(even_x, last, first)
    x_second_ref[0] = jnp.where(even_x, first, last)
    counts_copy.wait()
    counts = counts_s[...].astype(F32)
    x_first_ref[1] = counts
    x_second_ref[1] = counts
    low, high = counts[0:8, :], counts[height - 8 : height, :]
    for start in (0, 8 + 2 * levels):
        y_first_ref[start : start + 8, :] = jnp.where(even_y, high, low)
        y_second_ref[start : start + 8, :] = jnp.where(even_y, low, high)


def pack_tracers_kernel(first_kind, tracers_ref, *refs):
    x_first_ref, x_second_ref, y_first_ref, y_second_ref = refs[-4:]
    total, levels, height, width = tracers_ref.shape
    kinds = x_first_ref.shape[0] - first_kind
    even_x, even_y = is_even("gx"), is_even("gy")

    flat = tracers_ref.reshape(total * levels * height, width)
    for before_ref, ref in zip(refs[:-4], refs[-4:]):
        ref[0:first_kind] = before_ref[...]

    def one_kind(kind, carry):
        place = first_kind + kind

        for side_row in range(2):
            for start in range(0, levels - 8, 8):
                base = (place * levels + start) * height + side_row
                high = flat[pl.ds(base + height - 2, 8, stride=height), :]
                low = flat[pl.ds(base, 8, stride=height), :]
                tile = pl.ds(side_row * levels + start, 8)
                y_first_ref[place, tile, :] = jnp.where(even_y, high, low)
                y_second_ref[place, tile, :] = jnp.where(even_y, low, high)
        for level in range(levels - 8, levels):
            for side_row in range(2):
                at = height - 2 + side_row
                high = tracers_ref[place, level, at : at + 1, :]
                low = tracers_ref[place, level, side_row : side_row + 1, :]
                into = side_row * levels + level
                y_first_ref[place, into : into + 1, :] = jnp.where(even_y, high, low)
                y_second_ref[place, into : into + 1, :] = jnp.where(even_y, low, high)
        last, first = pack_columns(lambda level: tracers_ref[place, level], levels)
        x_first_ref[place] = jnp.where(even_x, last, first)
        x_second_ref[place] = jnp.where(even_x, first, last)
        return carry

    lax.fori_loop(0, kinds, one_kind, 0)


def pack_tracers(tracers, first_kind, count, before=()):
    kinds, levels, height, width = tracers.shape
    upto = first_kind + count
    return pl.pallas_call(
        functools.partial(pack_tracers_kernel, first_kind),
        in_specs=[vmem()] * (1 + len(before)),
        out_shape=[struct(upto, height, width)] * 2 + [struct(upto, 2 * levels, width)] * 2,
        compiler_params=params(20),
        cost_estimate=pl.CostEstimate(flops=10_000_000, bytes_accessed=6_000_000, transcendentals=0),
    )(tracers, *before)


def weights_of(level, mixing, tile, masks_ref, u, v):
    u8, u1 = u * (8.0 / 12.0), u * (1.0 / 12.0)
    v8, v1 = v * (8.0 / 12.0), v * (1.0 / 12.0)
    plain = (mixing - u8, mixing + u8, u1, -u1, mixing - v8, mixing + v8, v1, -v1)
    height = level.astype(F32)
    out = [jnp.where(height < masks_ref[at, tile, :], plain[at], 0.0) for at in range(8)]
    total = out[0]
    for weight in out[1:]:
        total = total + weight
    return out, 1.0 - total


def stencil(weights, own, tile_at, tiles, load_at, side, north_1, north_2, south_1, south_2):
    column = lanes(own.shape)
    row = rows(own.shape)
    base = 8 * tile_at
    width = own.shape[1]
    if tile_at + 1 < tiles:
        n1, n2 = load_at(base + 1), load_at(base + 2)
    else:
        n1 = jnp.where(row == 7, north_1(), roll(own, -1, 0))
        n2 = jnp.where(row >= 6, north_2(), roll(own, -2, 0))
    if tile_at > 0:
        s1, s2 = load_at(base - 1), load_at(base - 2)
    else:
        s1 = jnp.where(row == 0, south_1(), roll(own, 1, 0))
        s2 = jnp.where(row < 2, south_2(), roll(own, 2, 0))
    near, middle = weights
    total = middle * own
    for weight, value in zip(
        near,
        (
            roll(jnp.where(column < 1, side, own), -1, 1),
            roll(jnp.where(column >= width - 1, side, own), 1, 1),
            roll(jnp.where(column < 2, side, own), -2, 1),
            roll(jnp.where(column >= width - 2, side, own), 2, 1),
            n1,
            s1,
            n2,
            s2,
        ),
    ):
        total = total + weight * value
    return total


def table_parts(tables_ref, levels):
    planes, height, width = tables_ref.shape
    flat = tables_ref.reshape(planes * height, width)
    start = 9 * height
    return flat.at[pl.ds(start, height + 16)], flat.at[pl.ds(start + height + 16, levels)]


def forcing_kernel(
    b_ref,
    counts_ref,
    u_ref,
    v_ref,
    depth_ref,
    lat_ref,
    thick_ref,
    surface_ref,
    pressure_ref,
    x_first_ref,
    x_second_ref,
    y_first_ref,
    y_second_ref,
    fields_ref,
    masks_ref,
    sides_s,
    north_s,
    south_s,
):
    levels, height, width = b_ref.shape
    tiles = height // 8
    half = levels // 2
    counts_s, depths_ref = table_parts(masks_ref, levels)
    gx, gy = lax.axis_index("gx"), lax.axis_index("gy")
    even_x, even_y = is_even("gx"), is_even("gy")
    end_x, end_y = lax.axis_size("gx") - 1, lax.axis_size("gy") - 1
    counts = counts_ref[...].astype(F32)
    column = lanes(counts.shape)
    east = jnp.where(even_x, x_first_ref[1], x_second_ref[1]) * jnp.where(gx < end_x, 1.0, 0.0)
    west = jnp.where(even_x, x_second_ref[1], x_first_ref[1]) * jnp.where(gx > 0, 1.0, 0.0)
    north_s[...] = jnp.where(even_y, y_first_ref[...], y_second_ref[...])
    south_s[...] = jnp.where(even_y, y_second_ref[...], y_first_ref[...])
    masks_ref[0] = jnp.minimum(counts, roll(jnp.where(column < 1, east, counts), -1, 1))
    masks_ref[1] = jnp.minimum(counts, roll(jnp.where(column >= width - 1, west, counts), 1, 1))
    masks_ref[2] = jnp.minimum(counts, roll(jnp.where(column < 2, east, counts), -2, 1))
    masks_ref[3] = jnp.minimum(counts, roll(jnp.where(column >= width - 2, west, counts), 2, 1))
    counts_s[0:8, :] = south_s[0:8, :] * jnp.where(gy > 0, 1.0, 0.0)
    counts_s[8 : 8 + height, :] = counts
    counts_s[8 + height : 16 + height, :] = north_s[0:8, :] * jnp.where(gy < end_y, 1.0, 0.0)
    masks_ref[4] = jnp.minimum(counts, counts_s[9 : 9 + height, :])
    masks_ref[5] = jnp.minimum(counts, counts_s[7 : 7 + height, :])
    masks_ref[6] = jnp.minimum(counts, counts_s[10 : 10 + height, :])
    masks_ref[7] = jnp.minimum(counts, counts_s[6 : 6 + height, :])
    for level in range(levels):
        depths_ref[level : level + 1, :] = jnp.full((1, width), depth_ref[level], F32)
    row = rows(counts.shape)
    lat = jnp.zeros(counts.shape, F32)
    for at in range(height):
        lat = jnp.where(row == at, lat_ref[at], lat)
    masks_ref[8] = lat
    groups = unpack_groups(
        jnp.where(even_x, x_second_ref[0], x_first_ref[0]), jnp.where(even_x, x_first_ref[0], x_second_ref[0])
    )
    for level in range(levels):
        sides_s[level] = roll(groups[level // half], 126 - 4 * (level % half), 1)

    def level_body(level, carry):
        thick = thick_ref[level]
        forcing, depth_sum = list(carry[0]), list(carry[1])
        for tile_at in range(tiles):
            tile = pl.ds(8 * tile_at, 8)
            mixing = depth_ref[level] * masks_ref[8, tile, :]
            weights = weights_of(level, mixing, tile, masks_ref, u_ref[level, tile, :], v_ref[level, tile, :])
            value = stencil(
                weights,
                b_ref[level, tile, :],
                tile_at,
                tiles,
                lambda start: b_ref[level, pl.ds(start, 8), :],
                sides_s[level, tile, :],
                lambda: north_s[pl.ds(2 * level + 1, 8), :],
                lambda: north_s[pl.ds(2 * level + 2, 8), :],
                lambda: south_s[pl.ds(2 * level + 9, 8), :],
                lambda: south_s[pl.ds(2 * level + 8, 8), :],
            )
            weight = jnp.where(level.astype(F32) < counts_s[pl.ds(8 + 8 * tile_at, 8), :], thick, 0.0)
            forcing[tile_at] = forcing[tile_at] + weight * value
            depth_sum[tile_at] = depth_sum[tile_at] + weight
        return tuple(forcing), tuple(depth_sum)

    zeros = tuple(jnp.zeros((8, width), F32) for _ in range(tiles))
    forcing, depth_sum = lax.fori_loop(0, levels, level_body, (zeros, zeros), unroll=4)
    for at in range(tiles):
        tile = pl.ds(8 * at, 8)
        ocean = jnp.where(counts_s[pl.ds(8 + 8 * at, 8), :] > 0.0, 1.0, 0.0)
        fields_ref[0, tile, :] = ocean * (0.5 * forcing[at] + surface_ref[tile, :])
        fields_ref[1, tile, :] = pressure_ref[tile, :]
        fields_ref[2, tile, :] = 5.0 + 2.0 / (1.0 + depth_sum[at])


def shift_matrix():
    shape = (256, 256)
    column = lanes(shape)
    offset = rows(shape) % 128 - column % 128
    near = jnp.where(offset == 1, 1.0, 0.0)
    far = jnp.where(offset == -1, 1.0, 0.0)
    both = jnp.where(offset == 2, 1.0, 0.0) - jnp.where(offset == -2, 1.0, 0.0)
    return jnp.where(column < 128, near + far, 8.0 * (near - far) - both).astype(jnp.bfloat16)


def side_weights_kernel(masks_ref, u_ref, weights_ref):
    levels, height, width = u_ref.shape
    half = levels // 2
    depths_ref = table_parts(masks_ref, levels)[1]
    column = lanes((height, width))
    for group in range(2):
        near, far = jnp.zeros((height, width), F32), jnp.zeros((height, width), F32)
        for at in range(half):
            level = group * half + at
            mixing = depths_ref[level : level + 1, :] * masks_ref[8]
            u8, u1 = u_ref[level] * (8.0 / 12.0), u_ref[level] * (1.0 / 12.0)
            first = jnp.where(
                column == width - 1,
                jnp.where(level < masks_ref[0], mixing - u8, 0.0),
                jnp.where(level < masks_ref[1], mixing + u8, 0.0),
            )
            first = jnp.where((column == 0) | (column == width - 1), first, 0.0)
            second = jnp.where(
                column < 2, jnp.where(level < masks_ref[3], -u1, 0.0), jnp.where(level < masks_ref[2], u1, 0.0)
            )
            here = column // 4 == at
            near = jnp.where(here, roll(first, 4 * at - 126, 1), near)
            far = jnp.where(here, roll(second, 4 * at - 126, 1), far)
        weights_ref[group, 0] = near
        weights_ref[group, 1] = far


def side_kernel(weights_ref, x_first_ref, x_second_ref, sides_ref):
    kinds, height, width = x_first_ref.shape
    even_x = is_even("gx")
    spot = lanes((height, width)) % 4
    for kind in range(kinds):
        x_first, x_second = x_first_ref[kind], x_second_ref[kind]
        groups = unpack_groups(jnp.where(even_x, x_second, x_first), jnp.where(even_x, x_first, x_second))
        for group, values in enumerate(groups):
            by_two = jnp.where(spot < 2, roll(values, -2, 1), roll(values, 2, 1))
            by_one = jnp.where(spot < 2, roll(values, -1, 1), roll(values, 1, 1))
            sides_ref[kind, group] = weights_ref[group, 0] * by_one + weights_ref[group, 1] * by_two


def advance_kernel(
    tracers_ref,
    u_ref,
    v_ref,
    masks_ref,
    sides_ref,
    y_first_ref,
    y_second_ref,
    out_ref,
    held,
    masked_s,
    parts_s,
    moved_s,
    matrix_s,
    weights_s,
    north_s,
    south_s,
    in_semaphore,
    out_semaphore,
):
    kinds, levels, height, width = tracers_ref.shape
    groups = in_semaphore.shape[0]
    chunk = levels // groups
    tiles = height // 8
    half = levels // 2
    counts_ref, depths_ref = table_parts(masks_ref, levels)

    def load(group):
        where = (slice(None), pl.ds(group * chunk, chunk))
        return pltpu.make_async_copy(tracers_ref.at[where], held.at[where], in_semaphore.at[group])

    def store(group):
        where = (slice(None), pl.ds(group * chunk, chunk))
        return pltpu.make_async_copy(held.at[where], out_ref.at[where], out_semaphore.at[group])

    for group in range(groups):
        load(group).start()
    matrix_s[...] = shift_matrix()
    even_y = is_even("gy")
    for side_row in range(2):
        south_counts = counts_ref[6 + side_row : 7 + side_row, :]
        north_counts = counts_ref[8 + height + side_row : 9 + height + side_row, :]
        for start in range(0, levels, 8):
            number = (rows((8, width)) + start).astype(F32)
            in_north, in_south = number < north_counts, number < south_counts
            tile = pl.ds(side_row * levels + start, 8)
            for kind in range(kinds):
                first, second = y_first_ref[kind, tile, :], y_second_ref[kind, tile, :]
                into = pl.ds(2 * (kind * levels + start) + side_row, 8, stride=2)
                north_s[into, :] = jnp.where(in_north, jnp.where(even_y, first, second), 0.0)
                south_s[into, :] = jnp.where(in_south, jnp.where(even_y, second, first), 0.0)
    column = lanes((8, width))
    outer = (column < 2) | (column >= width - 2)

    def prepare(level, at):
        number = level.astype(F32)
        for tile_at in range(tiles):
            tile = pl.ds(8 * tile_at, 8)
            mixing = depths_ref[pl.ds(level, 1), :] * masks_ref[8, tile, :]
            u, v = u_ref[level, tile, :], v_ref[level, tile, :]
            active = number < counts_ref[pl.ds(8 + 8 * tile_at, 8), :]
            weights_s[at, 0, tile, :] = weights_of(level, mixing, tile, masks_ref, u, v)[1]
            weights_s[at, 1, tile, :] = jnp.where(active, mixing, 0.0)
            weights_s[at, 2, tile, :] = jnp.where(active, u * (-1.0 / 12.0), 0.0)
            weights_s[at, 3, tile, :] = jnp.where(active, v * (-1.0 / 12.0), 0.0)
        active = number < counts_ref[8 : 8 + height, :]
        for kind in range(kinds):
            seen = jnp.where(active, held[kind, level], 0.0)
            masked_s[at, kind, 8 : 8 + height, :] = seen
            high = seen.astype(jnp.bfloat16)
            row = (at * kinds + kind) * height
            parts_s[row : row + height, 0:width] = high
            parts_s[row : row + height, width : 2 * width] = (seen - high.astype(F32)).astype(jnp.bfloat16)
            masked_s[at, kind, 8 + height : 10 + height, :] = north_s[pl.ds(2 * (kind * levels + level), 2), :]
            masked_s[at, kind, 6:8, :] = south_s[pl.ds(2 * (kind * levels + level), 2), :]

    def finish(level, at):
        group = level // half
        shift = 126 - 4 * (level - half * group)
        for tile_at in range(tiles):
            base = 8 * tile_at
            tile = pl.ds(base, 8)
            own_weight, mixing, eastward, northward = (weights_s[at, i, tile, :] for i in range(4))
            for kind in range(kinds):
                row = (at * kinds + kind) * height + base
                n1, s1, n2, s2 = (masked_s[at, kind, pl.ds(8 + base + by, 8), :] for by in (1, -1, 2, -2))
                side = jnp.where(outer, pltpu.roll(sides_ref[kind, group, tile, :], shift, 1), 0.0)
                held[kind, level, tile, :] = (
                    own_weight * held[kind, level, tile, :]
                    + mixing * (moved_s[row : row + 8, 0:width] + (n1 + s1))
                    + eastward * moved_s[row : row + 8, width : 2 * width]
                    + northward * (8.0 * (n1 - s1) - (n2 - s2))
                    + side
                )

    def one_group(group, carry):
        load(group).wait()
        for at in range(chunk):
            prepare(group * chunk + at, at)
        moved_s[...] = jnp.dot(parts_s[...], matrix_s[...], preferred_element_type=F32)
        for at in range(chunk):
            finish(group * chunk + at, at)
        store(group).start()
        return carry

    lax.fori_loop(0, groups, one_group, 0)
    for group in range(groups):
        store(group).wait()


def outer_rows_kernel(fields_ref, x_first_ref, x_second_ref, side_ref, y_first_ref, y_second_ref):
    count, height, width = fields_ref.shape
    even_x, even_y = is_even("gx"), is_even("gy")
    eastern = (lanes((height, width)) < width // 2) == even_x
    for at in range(count):
        side = jnp.where(eastern, x_first_ref[at], x_second_ref[at])
        side_ref[at] = side
        for place, values in ((at, fields_ref[at]), (count + at, side)):
            low, high = values[0:8, :], values[height - 8 : height, :]
            y_first_ref[place] = jnp.where(even_y, high, low)
            y_second_ref[place] = jnp.where(even_y, low, high)


def extended(fields_ref, side_ref, y_first_ref, y_second_ref, at):
    count = fields_ref.shape[0]
    even_y = is_even("gy")

    def column(inner, place):
        first, second = y_first_ref[place], y_second_ref[place]
        return jnp.concatenate([inner, jnp.where(even_y, first, second), jnp.where(even_y, second, first)], axis=0)

    return jnp.concatenate([column(fields_ref[at], at), column(side_ref[at], count + at)], axis=1)


def krylov_kernel(fields_ref, side_ref, y_first_ref, y_second_ref, basis_ref, sums_ref):
    height, width = fields_ref.shape[1], fields_ref.shape[2]
    forcing, pressure, center = (
        extended(fields_ref, side_ref, y_first_ref, y_second_ref, at) for at in range(3)
    )
    shape = forcing.shape
    column, row = lanes(shape), rows(shape)
    gx, gy = lax.axis_index("gx"), lax.axis_index("gy")
    end_x, end_y = lax.axis_size("gx") - 1, lax.axis_size("gy") - 1
    least_column = jnp.where(gx < end_x, 0, width)
    most_column = jnp.where(gx > 0, 2 * width, width + width // 2)
    least_row = jnp.where(gy < end_y, 0, height)
    most_row = jnp.where(gy > 0, height + 16, height + 8)
    inside_x = (column < width) | ((column >= least_column) & (column < width + width // 2) & (gx < end_x)) | (
        (column >= width + width // 2) & (column < most_column)
    )
    inside_y = (row < height) | ((row >= least_row) & (row < height + 8) & (gy < end_y)) | (
        (row >= height + 8) & (row < most_row)
    )
    ocean = jnp.where((center < 6.75) & inside_x & inside_y, 1.0, 0.0)
    diagonal = jnp.where(ocean > 0.0, center, 1.0)

    def operate(values):
        seen = ocean * values
        beside = roll(seen, 1, 1) + roll(seen, -1, 1)
        mixed = seen + 0.25 * beside
        return diagonal * values - ocean * (beside + (roll(mixed, 1, 0) + roll(mixed, -1, 0)))

    def scaled(values):
        return 0.2 * operate(values) - values

    base = [forcing - operate(pressure)]
    base.append(scaled(base[0]))
    base.append(2.0 * scaled(base[1]) - base[0])
    base.append(2.0 * scaled(base[2]) - base[1])
    last = scaled(base[3])
    for at in range(4):
        basis_ref[at] = base[at]
    basis_ref[4] = pressure
    basis_ref[5] = ocean
    inner = [values[0:height, 0:width] for values in base]
    sums = []
    for at in range(4):
        for other in range(at + 1):
            sums.append(inner[at] * inner[other])
    sums.append(inner[3] * last[0:height, 0:width])
    line = jnp.zeros((8, width), F32)
    for at, values in enumerate(sums):
        part = values[0:8]
        for start in range(8, height, 8):
            part = part + values[start : start + 8]
        total = jnp.sum(jnp.sum(part, axis=0, keepdims=True), axis=1, keepdims=True)
        line = jnp.where(lanes(line.shape) == at, total, line)
    for start in range(0, sums_ref.shape[0], 8):
        sums_ref[start : start + 8, :] = line


def finish_kernel(basis_ref, sums_ref, pressure_ref, gradient_ref):
    height, width = pressure_ref.shape
    part = sums_ref[0:8, :]
    for start in range(8, sums_ref.shape[0], 8):
        part = part + sums_ref[start : start + 8, :]
    line = jnp.sum(part, axis=0, keepdims=True)

    def entry(at):
        return jnp.sum(jnp.where(lanes(line.shape) == at, line, 0.0), axis=1, keepdims=True)

    gram = [[None] * 4 for _ in range(4)]
    at = 0
    for i in range(4):
        for j in range(i + 1):
            gram[i][j] = gram[j][i] = entry(at)
            at += 1
    tail = entry(at)

    def scaled(coef):
        out = [None] * 5
        for j, value in enumerate(coef):
            if value is None:
                continue
            moves = [(1, value)] if j == 0 else [(j + 1, 0.5 * value), (j - 1, 0.5 * value)]
            for place, amount in moves:
                out[place] = amount if out[place] is None else out[place] + amount
        return out

    def dot(left, right):
        total = None
        for i in range(4):
            for j in range(4):
                if left[i] is None or right[j] is None:
                    continue
                term = left[i] * right[j] * gram[i][j]
                total = term if total is None else total + term
        return total

    def plus(left, factor, right):
        out = []
        for a, b in zip(left, right):
            if b is None:
                out.append(a)
            elif a is None:
                out.append(factor * b)
            else:
                out.append(a + factor * b)
        return out

    one = jnp.ones_like(tail)
    residual = [one, None, None, None]
    direction = [one, None, None, None]
    solution_coef = [None] * 4
    norm = dot(residual, residual)
    for step in range(ITERS):
        moved = scaled(direction)
        if step < ITERS - 1:
            energy = dot(direction, moved[:4])
        else:
            low = direction[:3] + [None]
            moved_low = scaled(low)[:4]
            energy = (
                dot(low, moved_low)
                + 2.0 * direction[3] * dot([None, None, None, one], moved_low)
                + direction[3] * direction[3] * tail
            )
        energy = 5.0 * (energy + dot(direction, direction))
        factor = norm / energy
        solution_coef = plus(solution_coef, factor, direction)
        if step < ITERS - 1:
            image = plus([None if m is None else 5.0 * m for m in moved[:4]], 5.0, direction)
            residual = plus(residual, -factor, image)
            new = dot(residual, residual)
            direction = plus(residual, new / norm, direction)
            norm = new

    pressure = basis_ref[4]
    for j in range(4):
        pressure = pressure + solution_coef[j] * basis_ref[j]
    ocean = basis_ref[5]
    seen = ocean * pressure
    half = 0.5 * ocean
    east = half * (roll(seen, -1, 1) - roll(seen, 1, 1))
    north = half * (roll(seen, -1, 0) - roll(seen, 1, 0))
    pressure_ref[...] = pressure[0:height, 0:width]
    gradient_ref[0] = east[0:height, 0:width]
    gradient_ref[1] = north[0:height, 0:width]


def exchange(first, second, axis):
    wide, tall = lax.axis_size("gx"), lax.axis_size("gy")
    pairs, others = [], []
    for x in range(wide):
        for y in range(tall):
            at = x * tall + y
            if axis == "gx":
                pairs.append((at, (x ^ 1) * tall + y))
                others.append((at, ((x + 1 if x % 2 else x - 1) % wide) * tall + y))
            else:
                pairs.append((at, x * tall + (y ^ 1)))
                beyond = y + 1 if y % 2 else y - 1
                inside = 0 <= beyond < tall
                others.append((at, x * tall + beyond if inside else (x ^ 1) * tall + y))
    return lax.ppermute(first, AXES, pairs), lax.ppermute(second, AXES, others)


def full(shape):
    return pl.BlockSpec(shape, lambda *_: (0,) * len(shape))


def vmem():
    return pl.BlockSpec(memory_space=pltpu.VMEM)


def hbm():
    return pl.BlockSpec(memory_space=pltpu.HBM)


def smem():
    return pl.BlockSpec(memory_space=pltpu.SMEM)


def params(limit=32, **more):
    return pltpu.CompilerParams(vmem_limit_bytes=limit * MIB, **more)


def struct(*shape):
    return jax.ShapeDtypeStruct(shape, F32)


def per_device(
    tracers,
    level_counts,
    u_vel,
    v_vel,
    diff_depth,
    diff_lat,
    thickness,
    surface_forcing,
    initial_pressure,
):
    kinds, levels, height, width = tracers.shape
    packed = 2 * levels
    with jax.named_scope("pack_buoyancy"):
        buoyancy, x_first, x_second, y_first, y_second = pl.pallas_call(
            pack_buoyancy_kernel,
            in_specs=[hbm(), hbm()],
            out_shape=[
                struct(levels, height, width),
                struct(2, height, width),
                struct(2, height, width),
                struct(packed + 16, width),
                struct(packed + 16, width),
            ],
            scratch_shapes=[
                pltpu.VMEM((2, levels, height, width), F32),
                pltpu.VMEM((height, width), jnp.int32),
                pltpu.SemaphoreType.DMA((8,)),
                pltpu.SemaphoreType.DMA,
            ],
            compiler_params=params(52),
        )(tracers, level_counts)
        u_vel, v_vel, surface_forcing, initial_pressure, x_first = lax.optimization_barrier(
            (u_vel, v_vel, surface_forcing, initial_pressure, x_first)
        )
    with jax.named_scope("buoyancy_halo"):
        x_halo = exchange(x_first, x_second, "gx")
        y_halo = exchange(y_first, y_second, "gy")
    with jax.named_scope("pack_tracers"):
        early = kinds // 2
        later, _ = lax.optimization_barrier((tracers, x_first))
        packs = pack_tracers(later, 0, early)
        buoyancy, *packs = lax.optimization_barrier((buoyancy, *packs))
    with jax.named_scope("forcing"):
        fields, masks = pl.pallas_call(
            forcing_kernel,
            in_specs=[vmem()] * 4 + [smem()] * 3 + [vmem()] * 6,
            out_shape=[struct(3, height, width), struct(12, height, width)],
            scratch_shapes=[
                pltpu.VMEM((levels, height, width), F32),
                pltpu.VMEM((packed + 16, width), F32),
                pltpu.VMEM((packed + 16, width), F32),
            ],
            compiler_params=params(8),
        )(
            buoyancy,
            level_counts,
            u_vel,
            v_vel,
            diff_depth,
            diff_lat,
            thickness,
            surface_forcing,
            initial_pressure,
            *x_halo,
            *y_halo,
        )
    with jax.named_scope("fields_halo"):
        f_x_halo = exchange(fields, fields, "gx")
        later, _ = lax.optimization_barrier((tracers, fields))
        packs = pack_tracers(later, early, kinds - early, packs)
        own_fields, *packs = lax.optimization_barrier((fields, *packs))
        side, f_y_first, f_y_second = pl.pallas_call(
            outer_rows_kernel,
            out_shape=[struct(3, height, width), struct(6, 8, width), struct(6, 8, width)],
            compiler_params=params(4),
        )(own_fields, *f_x_halo)
        f_y_halo = exchange(f_y_first, f_y_second, "gy")
        masks, _ = lax.optimization_barrier((masks, f_y_first))
        side_weights = pl.pallas_call(
            side_weights_kernel,
            out_shape=struct(2, 2, height, width),
            compiler_params=params(8),
            cost_estimate=pl.CostEstimate(flops=2_000_000, bytes_accessed=2_000_000, transcendentals=0),
        )(masks, u_vel)
    with jax.named_scope("tracer_halo"):
        t_x_first, t_x_second, t_y_first, t_y_second = packs
        t_x_halo = exchange(t_x_first, t_x_second, "gx")
        *f_y_halo, t_y_first, t_y_second = lax.optimization_barrier((*f_y_halo, t_y_first, t_y_second))
        t_y_halo = exchange(t_y_first, t_y_second, "gy")
    with jax.named_scope("krylov"):
        basis, sums = pl.pallas_call(
            krylov_kernel,
            out_shape=[struct(6, height + 16, 2 * width), struct(128, width)],
            compiler_params=params(8),
        )(fields, side, *f_y_halo)
        all_sums = lax.all_to_all(sums, AXES, 0, 0, tiled=True)
    with jax.named_scope("side_terms"):
        side_weights, _ = lax.optimization_barrier((side_weights, sums))
        sides = pl.pallas_call(
            side_kernel,
            out_shape=struct(kinds, 2, height, width),
            compiler_params=params(8),
            cost_estimate=pl.CostEstimate(flops=4_000_000, bytes_accessed=3_000_000, transcendentals=0),
        )(side_weights, *t_x_halo)
    chunk = 4
    with jax.named_scope("advance"):
        new_tracers = pl.pallas_call(
            advance_kernel,
            in_specs=[hbm()] + [vmem()] * 6,
            out_specs=hbm(),
            out_shape=struct(kinds, levels, height, width),
            scratch_shapes=[
                pltpu.VMEM((kinds, levels, height, width), F32),
                pltpu.VMEM((chunk, kinds, height + 16, width), F32),
                pltpu.VMEM((chunk * kinds * height, 2 * width), jnp.bfloat16),
                pltpu.VMEM((chunk * kinds * height, 2 * width), F32),
                pltpu.VMEM((2 * width, 2 * width), jnp.bfloat16),
                pltpu.VMEM((chunk, 4, height, width), F32),
                pltpu.VMEM((kinds * packed + 8, width), F32),
                pltpu.VMEM((kinds * packed + 8, width), F32),
                pltpu.SemaphoreType.DMA((levels // chunk,)),
                pltpu.SemaphoreType.DMA((levels // chunk,)),
            ],
            compiler_params=params(52),
            cost_estimate=pl.CostEstimate(flops=60_000_000, bytes_accessed=22_000_000, transcendentals=0),
        )(tracers, u_vel, v_vel, masks, sides, *t_y_halo)
    with jax.named_scope("solve"):
        new_tracers, all_sums = lax.optimization_barrier((new_tracers, all_sums))
        pressure, gradient = pl.pallas_call(
            finish_kernel,
            out_shape=[struct(height, width), struct(2, height, width)],
            compiler_params=params(8),
        )(basis, all_sums)
    return new_tracers, pressure, gradient


def solution(mesh):
    return jax.shard_map(
        per_device,
        mesh=mesh,
        in_specs=(
            P(None, None, "gy", "gx"),
            P("gy", "gx"),
            P(None, "gy", "gx"),
            P(None, "gy", "gx"),
            P(),
            P("gy"),
            P(),
            P("gy", "gx"),
            P("gy", "gx"),
        ),
        out_specs=(P(None, None, "gy", "gx"), P("gy", "gx"), P(None, "gy", "gx")),
        check_vma=False,
    )
```
